128 devices in a mesh: fsdp: 32 (over z, x, core), seq: 4 (over y).
Axes of the slice: x: 4, y: 4, z: 4, core: 2. Of those that a mesh axis runs over, the one named last changes fastest.
Arguments:
- tokens: bfloat16 [49152, 768], P(('fsdp', 'seq')), may hold values from -24 to 24
- slot_seq: int32 [384], P('fsdp'), may hold values from 0 to 2, as said below
- slot_block_index: int32 [384], P('fsdp'), may hold values from 0 to 7
- lengths: int32 [32, 3], P('fsdp'), may hold values from 1 to 1024, as said below
- ln1_gain: bfloat16 [768], P(('fsdp', 'seq')), may hold values from 0.25 to 1.75
- ln1_bias: bfloat16 [768], P(('fsdp', 'seq')), may hold values from -1.75 to 1.75
- w_qkv: bfloat16 [768, 2304], P(('fsdp', 'seq')), may hold values from -0.21875 to 0.21875
- qv_bias: bfloat16 [1536], P(('fsdp', 'seq')), may hold values from -0.625 to 0.625
- w_out: bfloat16 [768, 768], P(('fsdp', 'seq')), may hold values from -1.75 to 1.75
- out_bias: bfloat16 [768], P(('fsdp', 'seq')), may hold values from -1.75 to 1.75
- ln2_gain: bfloat16 [768], P(('fsdp', 'seq')), may hold values from 0.25 to 1.75
- ln2_bias: bfloat16 [768], P(('fsdp', 'seq')), may hold values from -1.75 to 1.75
- w_fc: bfloat16 [768, 3072], P(('fsdp', 'seq')), may hold values from -0.21875 to 0.21875
- feed_input_bias: bfloat16 [3072], P(('fsdp', 'seq')), may hold values from -3 to 3
- w_proj: bfloat16 [3072, 768], P(('fsdp', 'seq')), may hold values from -0.109375 to 0.109375
- proj_bias: bfloat16 [768], P(('fsdp', 'seq')), may hold values from -1.75 to 1.75
- cotangent: bfloat16 [49152, 768], P(('fsdp', 'seq')), may hold values from -6 to 6
Outputs:
- block_out: bfloat16 [49152, 768], P(('fsdp', 'seq'))
- tokens_grad: bfloat16 [49152, 768], P(('fsdp', 'seq'))
- ln1_gain_grad: float32 [768], P(('fsdp', 'seq'))
- ln1_bias_grad: float32 [768], P(('fsdp', 'seq'))
- w_qkv_grad: float32 [768, 2304], P(('fsdp', 'seq'))
- qv_bias_grad: float32 [1536], P(('fsdp', 'seq'))
- w_out_grad: float32 [768, 768], P(('fsdp', 'seq'))
- out_bias_grad: float32 [768], P(('fsdp', 'seq'))
- ln2_gain_grad: float32 [768], P(('fsdp', 'seq'))
- ln2_bias_grad: float32 [768], P(('fsdp', 'seq'))
- w_fc_grad: float32 [768, 3072], P(('fsdp', 'seq'))
- fc_bias_grad: float32 [3072], P(('fsdp', 'seq'))
- w_proj_grad: float32 [3072, 768], P(('fsdp', 'seq'))
- proj_bias_grad: float32 [768], P(('fsdp', 'seq'))
The draws below stay inside these ranges and needn't reach their ends.
Inputs may be any that keep to these rules, and one draw needn't show every extreme that they name: `slot_seq`: in each group every slot holds one block of one sequence; block b of a sequence covers its positions b * 128 to b * 128 + 127, and a sequence of length L has exactly (L + 127) // 128 blocks in its group, each in one slot. `lengths`: one sequence of each group has length 1024.
All inputs are finite; a program needn't handle non-finite values.
Results may differ from the reference program's by a relative error of at most 0.019.
Values may be sent and summed in bfloat16 or wider, within the bound.
No kernel may reach another device: no remote copies, remote signals or barrier semaphores. Data moves between devices by JAX's collectives and lax.ppermute only.
A program may use at most 128 MiB of HBM per device.

```python
import jax
import jax.numpy as jnp
from jax import lax

D = 768
H = 12
HD = 64
FF = 3072
BLK = 128
SLOTS = 3
NSEQ = 3
GROUPS = 32
GSLOTS = 12
BLOCK_TOTAL = 384
ROWS = 49152
LONG_BLK = 8


def group_layout(subkey):
    long_key, extra_key, placement_random_key, shuffle_key, pad_key = jax.random.split(subkey, 5)
    group_devices = GSLOTS // SLOTS
    longest = jax.random.randint(long_key, (), 0, NSEQ)
    spare_count = GSLOTS - LONG_BLK
    others = NSEQ - 1
    extra_picks = jax.random.randint(extra_key, (spare_count - others,), 0, others)
    other_ids = jnp.arange(others)
    other_counts = 1 + jnp.sum((extra_picks[:, None] == other_ids[None, :]).astype(jnp.int32), axis=0)
    other_ends = jnp.cumsum(other_counts)
    other_starts = other_ends - other_counts
    stream = jnp.arange(spare_count)
    owner_index = jnp.sum((stream[:, None] >= other_ends[None, :]).astype(jnp.int32), axis=1)
    owner_block = stream - other_starts[owner_index]
    owner_seq = owner_index + (owner_index >= longest).astype(jnp.int32)
    shuffle = jax.random.permutation(shuffle_key, spare_count)
    owner_seq = owner_seq[shuffle]
    owner_block = owner_block[shuffle]
    places = jax.vmap(lambda branch_key: jax.random.permutation(branch_key, SLOTS))(jax.random.split(placement_random_key, group_devices))
    device_ids = jnp.arange(group_devices)
    long_slots = (device_ids[:, None] * SLOTS + places[:, :2]).reshape(LONG_BLK)
    long_blocks = (device_ids[:, None] * 2 + jnp.arange(2)[None, :]).reshape(LONG_BLK)
    unused_slots = (device_ids[:, None] * SLOTS + places[:, 2:]).reshape(spare_count)
    seq_table = jnp.zeros((GSLOTS,), jnp.int32).at[long_slots].set(longest).at[unused_slots].set(owner_seq.astype(jnp.int32))
    block_table = jnp.zeros((GSLOTS,), jnp.int32).at[long_slots].set(long_blocks.astype(jnp.int32)).at[unused_slots].set(owner_block.astype(jnp.int32))
    seq_ids = jnp.arange(NSEQ)
    other_slot = jnp.clip(seq_ids - (seq_ids > longest).astype(jnp.int32), 0, others - 1)
    block_counts = jnp.where(seq_ids == longest, LONG_BLK, other_counts[other_slot])
    pad_counts = jax.random.randint(pad_key, (NSEQ,), 0, BLK)
    seq_lengths = block_counts * BLK - jnp.where(seq_ids == longest, 0, pad_counts)
    return (seq_table, block_table, seq_lengths.astype(jnp.int32))


def every_layout(key):
    base_key = jax.random.fold_in(key, 11)
    group_keys = jax.vmap(lambda group_index: jax.random.fold_in(base_key, group_index))(jnp.arange(GROUPS))
    return jax.vmap(group_layout)(group_keys)


def draw_slot_seq(key, part):
    return every_layout(key)[0].reshape(BLOCK_TOTAL).astype(jnp.int32)


def draw_slot_block_index(key, part):
    return every_layout(key)[1].reshape(BLOCK_TOTAL).astype(jnp.int32)


def draw_lengths(key, part):
    return every_layout(key)[2].reshape(GROUPS, NSEQ).astype(jnp.int32)


def with_spikes(drawn, stream_key, source, target, shards_of, factor):
    owner, partner = [(jnp.arange(drawn.shape[dim]) // (drawn.shape[dim] // shards_of)).reshape([-1 if axis == dim else 1 for axis in range(drawn.ndim)]) for dim in (source, target)]
    chosen = jax.random.permutation(stream_key, shards_of)[partner]
    strong = (owner == chosen) | (owner == (partner + shards_of // 2) % shards_of)
    return jnp.where(strong, factor * drawn, drawn)


def steps_of(stream_key, shape, cuts, low, top_value):
    def one(dim, blocks):
        draws = jax.random.uniform(jax.random.fold_in(jax.random.fold_in(stream_key, 6), dim), (blocks,), jnp.float32, low / len(cuts), top_value / len(cuts))
        return jnp.repeat(jnp.exp(draws), shape[dim] // blocks).reshape((-1,) + (1,) * (len(shape) - dim - 1))

    level = one(*cuts[0])
    for cut in cuts[1:]:
        level = level * one(*cut)
    return level


def bell_draw(stream_key, shape, deviation, reach, shards=(), kind=jnp.bfloat16):
    values = jax.random.normal(stream_key, shape, jnp.float32) * deviation
    if len(shards) > 0:
        values = steps_of(stream_key, shape, shards, -0.22, 0.18) * values
    return jnp.clip(values, min=-reach, max=reach).astype(kind)


def bell_draw_with(rng, dims, deviation, reach, cuts, heavy, kind=jnp.bfloat16):
    entries = deviation * jax.random.normal(rng, dims, jnp.float32)
    if cuts:
        entries = entries * steps_of(rng, dims, cuts, -0.22, 0.18)
    return jnp.clip(with_spikes(entries, jax.random.fold_in(rng, 3), *heavy), -reach, reach).astype(kind)


def setup_inputs(seed: int = 0) -> dict:
    seeds = jax.random.split(jax.random.key(seed), 18)
    return {
        "tokens": bell_draw_with(seeds[0], (ROWS, D), 1.0, 24.0, ((0, 128),), (0, 1, 128, 5.5)),
        "slot_seq": draw_slot_seq(jax.random.fold_in(seeds[17], 71), 0),
        "slot_block_index": draw_slot_block_index(jax.random.fold_in(seeds[17], 71), 0),
        "lengths": draw_lengths(jax.random.fold_in(seeds[17], 71), 0),
        "ln1_gain": jnp.clip(1.0 + 0.15 * jax.random.normal(seeds[4], (D,), jnp.float32), 0.25, 1.75).astype(jnp.bfloat16),
        "ln1_bias": bell_draw(seeds[5], (D,), 0.3, 1.75, ((0, 128),)),
        "w_qkv": bell_draw(seeds[6], (D, 3 * D), D ** -0.5, 0.21875, ((0, 128),)),
        "qv_bias": bell_draw(seeds[7], (2 * D,), 0.1, 0.625, ((0, 128),)),
        "w_out": bell_draw(seeds[8], (D, D), (D // 64) ** -0.5, 1.75, ((0, 128),)),
        "out_bias": bell_draw(seeds[9], (D,), 0.3, 1.75, ((0, 128),)),
        "ln2_gain": jnp.clip(1.0 + 0.15 * jax.random.normal(seeds[10], (D,), jnp.float32), 0.25, 1.75).astype(jnp.bfloat16),
        "ln2_bias": bell_draw(seeds[11], (D,), 0.3, 1.75, ((0, 128),)),
        "w_fc": bell_draw(seeds[12], (D, FF), D ** -0.5, 0.21875, ((0, 128),)),
        "feed_input_bias": bell_draw(seeds[13], (FF,), 0.5, 3.0, ((0, 128),)),
        "w_proj": bell_draw(seeds[14], (FF, D), FF ** -0.5, 0.109375, ((0, 128),)),
        "proj_bias": bell_draw(seeds[15], (D,), 0.3, 1.75, ((0, 128),)),
        "cotangent": bell_draw(seeds[16], (ROWS, D), 1.0, 6.0, ((0, 128),)),
    }


@jax.custom_vjp
def low(v):
    return lax.optimization_barrier(v.astype(jnp.bfloat16)).astype(jnp.float32)

@jax.custom_vjp
def low_back(v):
    return v

def low_keep(v):
    return (low(v), None)

def low_pass(kept, grad):
    return (grad,)

def back_keep(v):
    return (v, None)

def back_low(kept, grad):
    return (low(grad),)
low.defvjp(low_keep, low_pass)
low_back.defvjp(back_keep, back_low)
EPSILON = 1e-05
MASKED_SCORE = -1e+30
HIGHEST = lax.Precision.HIGHEST

def round_both(value):
    return low(low_back(value))

def normalized_rows(value, gain, shift):
    center = lax.optimization_barrier(jnp.mean(value, axis=-1, keepdims=True))
    offset = value - center
    spread = lax.optimization_barrier(jnp.mean(offset * offset, axis=-1, keepdims=True))
    return offset * lax.rsqrt(spread + EPSILON) * gain + shift

def group_forward(inputs, row_seq, row_pos, row_len, params):
    gain_one, shift_one, w_qkv, qv_bias, w_out, out_bias, gain_two, shift_two, w_fc, feed_input_bias, w_proj, proj_bias = params
    count = inputs.shape[0]
    acts_one = low(normalized_rows(inputs, gain_one, shift_one))
    joined = jnp.dot(acts_one, w_qkv, precision=HIGHEST)
    queries = round_both(joined[:, :D] + qv_bias[:D])
    key_rows = round_both(joined[:, D:2 * D])
    value_rows = round_both(joined[:, 2 * D:] + qv_bias[D:])
    query_heads = queries.reshape(count, H, HD)
    key_heads = key_rows.reshape(count, H, HD)
    value_heads = value_rows.reshape(count, H, HD)
    scores = low_back(jnp.einsum('qhd,khd->hqk', query_heads, key_heads, precision=HIGHEST) * HD ** (-0.5))
    visible = (row_seq[:, None] == row_seq[None, :]) & (row_pos[None, :] <= row_pos[:, None]) & (row_pos[None, :] < row_len[None, :])
    scores = jnp.where(visible[None], scores, MASKED_SCORE)
    top_score = lax.optimization_barrier(jnp.max(scores, axis=-1, keepdims=True))
    weights = jnp.exp(scores - top_score)
    probs = weights / lax.optimization_barrier(jnp.sum(weights, axis=-1, keepdims=True))
    mixed = jnp.einsum('hqk,khd->qhd', low(probs), value_heads, precision=HIGHEST).reshape(count, D)
    mixed = round_both(mixed)
    attn_out = low_back(jnp.dot(mixed, w_out, precision=HIGHEST) + out_bias)
    middle = inputs + attn_out
    acts_two = low(normalized_rows(middle, gain_two, shift_two))
    hidden = low_back(jnp.dot(acts_two, w_fc, precision=HIGHEST) + feed_input_bias)
    active = low(jax.nn.gelu(hidden, approximate=True))
    return middle + jnp.dot(active, w_proj, precision=HIGHEST) + proj_bias

def reference(tokens, slot_seq, slot_block_index, lengths, ln1_gain, ln1_bias, w_qkv, qv_bias, w_out, out_bias, ln2_gain, ln2_bias, w_fc, feed_input_bias, w_proj, proj_bias, cotangent):
    group_rows = GSLOTS * BLK
    inputs = tokens.astype(jnp.float32).reshape(GROUPS, group_rows, D)
    seq_table = slot_seq.reshape(GROUPS, GSLOTS)
    block_table = slot_block_index.reshape(GROUPS, GSLOTS)
    params = tuple((item.astype(jnp.float32) for item in (ln1_gain, ln1_bias, w_qkv, qv_bias, w_out, out_bias, ln2_gain, ln2_bias, w_fc, feed_input_bias, w_proj, proj_bias)))
    offsets = (jnp.arange(group_rows) % BLK).astype(jnp.int32)
    row_seq = jnp.repeat(seq_table, BLK, axis=1).astype(jnp.int32)
    row_pos = (jnp.repeat(block_table, BLK, axis=1) * BLK + offsets[None, :]).astype(jnp.int32)
    row_len = jnp.take_along_axis(lengths, row_seq, axis=1).astype(jnp.int32)
    live = (row_pos < row_len).astype(jnp.float32)

    def forward(values, weights_in):

        def group_step(pieces):
            return group_forward(pieces[0], pieces[1], pieces[2], pieces[3], weights_in)
        return lax.map(jax.checkpoint(group_step), (values, row_seq, row_pos, row_len))
    result, pullback = jax.vjp(forward, inputs, params)
    seed_grad = cotangent.astype(jnp.float32).reshape(GROUPS, group_rows, D) * live[:, :, None]
    input_grad, grads = pullback(seed_grad)
    return (result.reshape(ROWS, D).astype(jnp.bfloat16), input_grad.reshape(ROWS, D).astype(jnp.bfloat16), grads[0], grads[1], grads[2], grads[3], grads[4], grads[5], grads[6], grads[7], grads[8], grads[9], grads[10], grads[11])
```

```python
import numpy as np
import jax
import jax.numpy as jnp
from jax import lax
from jax.experimental import pallas as pl
from jax.experimental.pallas import tpu as pltpu
from jax.sharding import PartitionSpec as P

D = 768
H = 12
HD = 64
FF = 3072
BLK = 128
SLOTS = 3
NY = 4
GSLOTS = SLOTS * NY
ROWS = SLOTS * BLK
GROWS = GSLOTS * BLK
LONG = 8
LONG_LEN = LONG * BLK
HEADS = H // NY
HW = HEADS * HD
WQ = 3 * HW
QCOLS = 640
C_FC = 768
C_PROJ = C_FC + FF
C_VEC = C_PROJ + FF
WCOLS = C_VEC + 128
EPSILON = 1e-05
MASKED_SCORE = -1e30
SCALE = HD**-0.5
SEQ_STRIDE = 4096
M_INV, M_CODE, M_BASE, M_LIM, M_ZXY, M_THR = 0, 12, 16, 20, 24, 27
F32 = jnp.float32
BF16 = jnp.bfloat16
TILES = tuple((256 * t, 0, 256 * (t + 1)) for t in range(4)) + ((1024, 1024, 256), (1280, 1024, 512))


def dot_nn(a, b):
    return lax.dot_general(a, b, (((1,), (0,)), ((), ())), preferred_element_type=F32)


def dot_nt(a, b):
    return lax.dot_general(a, b, (((1,), (1,)), ((), ())), preferred_element_type=F32)


def dot_tn(a, b):
    return lax.dot_general(a, b, (((0,), (0,)), ((), ())), preferred_element_type=F32)


def normed(value):
    center = jnp.mean(value, axis=-1, keepdims=True)
    offset = value - center
    spread = jnp.mean(offset * offset, axis=-1, keepdims=True)
    scale = lax.rsqrt(spread + EPSILON)
    return offset * scale, scale


def minus(a, k, n):
    r = a - k
    return jnp.where(r < 0, r + n, r)


def visible_mask(meta, tile):
    q0, k0, count = tile
    row = lax.broadcasted_iota(jnp.int32, (256, 1), 0)
    col = lax.broadcasted_iota(jnp.int32, (1, count), 1)
    if q0 < LONG_LEN:
        return col <= row + q0
    first = (q0 - LONG_LEN) // BLK

    def per_slot(base, index, start, n):
        value = jnp.full(index.shape, meta[base + start], jnp.int32)
        for i in range(1, n):
            value = jnp.where(index >= i * BLK, meta[base + start + i], value)
        return value

    q_code = per_slot(M_CODE, row, first, 2) + (row & (BLK - 1))
    q_base = per_slot(M_BASE, row, first, 2)
    slots = count // BLK
    k_code = per_slot(M_CODE, col, 0, slots) + (col & (BLK - 1))
    k_lim = per_slot(M_LIM, col, 0, slots)
    k_code = jnp.where(k_code < k_lim, k_code, 1 << 24)
    return (k_code <= q_code) & (k_code >= q_base)


def select_matrix(r0, offset):
    rows = lax.broadcasted_iota(jnp.int32, (D, HW), 0)
    return jnp.where(rows == r0 + offset, 1.0, 0.0).astype(BF16)


def front_kernel(nz, nx, meta, *refs):
    x_refs, refs = refs[:NY], refs[NY:]
    z_refs, refs = refs[:nz], refs[nz:]
    r0_ref, k_ref = refs[:2]
    a1_ref, qkv_ref, lse_ref = refs[2:5]
    o_refs = refs[5 : 5 + NY]
    w_ref, gain_ref, oh = refs[5 + NY :]
    z, x, y = meta[M_ZXY], meta[M_ZXY + 1], meta[M_ZXY + 2]
    step = D // (nz * nx)
    for kz in range(nz):
        for kx in range(nx):
            at = (minus(z, kz, nz) * nx + minus(x, kx, nx)) * step
            w_ref[pl.ds(pl.multiple_of(at, step), step), :] = z_refs[kz][kx]
    vectors = jnp.transpose(w_ref[:, 512:640].astype(F32))
    gain = vectors[64:65]
    shift = vectors[65:66]
    gain_ref[...] = jnp.broadcast_to(gain, (8, D))
    small = vectors[64:72].astype(BF16)
    odd = k_ref[...] == 1
    sums = dot_nn(small, select_matrix(r0_ref[...], 96 * y))
    q_bias = jnp.where(odd, sums[3:4], sums[2:3])
    sums = dot_nn(small, select_matrix(r0_ref[...], 384 + 96 * y))
    v_bias = jnp.where(odd, sums[3:4], sums[2:3])
    bias = jnp.concatenate([q_bias, jnp.zeros((1, HW), F32), v_bias], axis=1)
    for k in range(NY):
        for j in range(SLOTS):
            hat, _ = normed(x_refs[k][j * BLK : (j + 1) * BLK, :].astype(F32))
            to = pl.multiple_of(meta[M_INV + k * SLOTS + j] * BLK, BLK)
            a1_ref[pl.ds(to, BLK), :] = (hat * gain + shift).astype(BF16)

    def project(t, carry):
        rows = pl.ds(pl.multiple_of(t * 256, 256), 256)
        joined = (dot_nn(a1_ref[rows, :], w_ref[:, 0:WQ]) + bias).astype(BF16)
        for i in range(9):
            qkv_ref[i, rows, :] = joined[:, i * HD : (i + 1) * HD]
        return carry

    lax.fori_loop(0, GROWS // 256, project, 0)

    def head(h, carry):
        for tile in TILES:
            q0, k0, count = tile
            q = qkv_ref[h, q0 : q0 + 256, :]
            k = qkv_ref[HEADS + h, k0 : k0 + count, :]
            v = qkv_ref[2 * HEADS + h, k0 : k0 + count, :]
            scores = jnp.where(visible_mask(meta, tile), dot_nt(q, k) * SCALE, MASKED_SCORE)
            top = jnp.max(scores, axis=-1, keepdims=True)
            weights = jnp.exp(scores - top)
            total = jnp.sum(weights, axis=-1, keepdims=True)
            probs = (weights * (1.0 / total)).astype(BF16)
            oh[h, q0 : q0 + 256, :] = dot_nn(probs, v)
            lse_ref[h, q0 : q0 + 256, :] = top + jnp.log(total)
        return carry

    lax.fori_loop(0, HEADS, head, 0)
    for k in range(NY):
        for j in range(SLOTS):
            rows = pl.ds(pl.multiple_of(meta[M_INV + k * SLOTS + j] * BLK, BLK), BLK)
            mixed = jnp.concatenate([oh[h, rows, :] for h in range(HEADS)], axis=1)
            o_refs[k][j * BLK : (j + 1) * BLK, :] = mixed.astype(BF16)


GELU_C = float(np.sqrt(2.0 / np.pi))


def middle_kernel(meta, *refs):
    o_refs, refs = refs[:NY], refs[NY:]
    x_ref, cot_ref, w_hbm = refs[:3]
    out_ref, dy_ref = refs[3:5]
    do_refs, refs = refs[5 : 5 + NY], refs[5 + NY :]
    g_hbm, w, g, mid, hat2, scale2, a2, a2t, dz, acc, acc_da, fcb, gvec, sems = refs
    y = meta[M_ZXY + 2]
    spans = ((0, C_FC), (C_VEC, 128), (C_FC, FF), (C_PROJ, FF))
    loads = [
        pltpu.make_async_copy(w_hbm.at[:, pl.ds(a, n)], w.at[:, pl.ds(a, n)], sems.at[i])
        for i, (a, n) in enumerate(spans)
    ]
    stores = [
        pltpu.make_async_copy(g.at[:, pl.ds(a, n)], g_hbm.at[:, pl.ds(a, n)], sems.at[4 + i])
        for i, (a, n) in enumerate(spans)
    ]
    for load in loads:
        load.start()
    offset = lax.broadcasted_iota(jnp.int32, (BLK, 1), 0)
    for j in range(SLOTS):
        rows = slice(j * BLK, (j + 1) * BLK)
        live = jnp.where(offset < meta[M_THR + j], 1.0, 0.0)
        dz[rows, :] = (cot_ref[rows, :].astype(F32) * live).astype(BF16)
    loads[0].wait()
    loads[1].wait()
    vectors = jnp.transpose(w[:, C_VEC : C_VEC + 128].astype(F32))
    out_bias, gain, shift, proj_bias = (vectors[i : i + 1] for i in range(4, 8))
    for c in range(12):
        q, s = divmod(c, 3)
        fcb[c] = jnp.broadcast_to(vectors[8 + q : 9 + q, s * 256 : (s + 1) * 256], (8, 256))
    sources = [pl.multiple_of(minus(y, k, NY) * HW, HW) for k in range(NY)]
    total = x_ref[...].astype(F32) + out_bias
    for k in range(NY):
        total = total + dot_nn(o_refs[k][...], w[pl.ds(sources[k], HW), 0:D])
    mid[...] = total
    hat, scale = normed(total)
    hat2[...] = hat
    scale2[...] = scale
    acts = hat * gain + shift
    a2[...] = acts.astype(BF16)
    a2t[...] = jnp.transpose(acts).astype(BF16)
    acc[...] = jnp.zeros_like(acc)
    acc_da[...] = jnp.zeros_like(acc_da)
    loads[2].wait()
    loads[3].wait()

    def chunk(c, carry):
        q = c // 3
        at_fc = pl.ds(pl.multiple_of(C_FC + 256 * c, 256), 256)
        at_p = pl.ds(pl.multiple_of(C_PROJ + D * q, 256), D)
        rows_p = pl.ds(pl.multiple_of(256 * (c - 3 * q), 256), 256)
        u = dot_nn(a2[...], w[:, at_fc]) + fcb[c][0:1]
        inner = GELU_C * (u + 0.044715 * (u * u * u))
        t = jnp.tanh(inner)
        m = (0.5 * u * (1.0 + t)).astype(BF16)
        slope = 0.5 * (1.0 + t) + (0.5 * GELU_C) * u * (1.0 - t * t) * (1.0 + 0.134145 * (u * u))
        p = w[rows_p, at_p]
        acc[...] += dot_nn(m, p)
        du32 = dot_nt(dz[...], p) * slope
        du = du32.astype(BF16)
        g[rows_p, at_p] = dot_tn(m, dz[...]).astype(BF16)
        g[:, at_fc] = dot_nn(a2t[...], du).astype(BF16)
        acc_da[...] += dot_nt(du, w[:, at_fc])
        fcb[c] = jnp.broadcast_to(jnp.sum(du.astype(F32), axis=0, keepdims=True), (8, 256))
        return carry

    lax.fori_loop(0, 12, chunk, 0)
    stores[2].start()
    stores[3].start()
    out_ref[...] = (mid[...] + acc[...] + proj_bias).astype(BF16)
    da2 = acc_da[...]
    gvec[...] = jnp.zeros_like(gvec)
    hat = hat2[...]
    gvec[6:7, :] = jnp.sum(da2, axis=0, keepdims=True)
    gvec[5:6, :] = jnp.sum(da2 * hat, axis=0, keepdims=True)
    dhat = da2 * gain
    mean_a = jnp.mean(dhat, axis=-1, keepdims=True)
    mean_b = jnp.mean(dhat * hat, axis=-1, keepdims=True)
    dz32 = dz[...].astype(F32)
    dy = dz32 + scale2[...] * (dhat - mean_a - hat * mean_b)
    dy_ref[...] = dy
    da = dy.astype(BF16)
    gvec[7:8, :] = jnp.sum(dz32, axis=0, keepdims=True)
    gvec[4:5, :] = jnp.sum(da.astype(F32), axis=0, keepdims=True)
    for q in range(4):
        for s in range(3):
            gvec[8 + q : 9 + q, s * 256 : (s + 1) * 256] = fcb[3 * q + s][0:1]
    for k in range(NY):
        do_refs[k][...] = dot_nt(da, w[pl.ds(sources[k], HW), 0:D]).astype(BF16)
        g[pl.ds(sources[k], HW), 0:D] = dot_tn(o_refs[k][...], da).astype(BF16)
    g[:, C_VEC : C_VEC + 128] = jnp.transpose(gvec[...]).astype(BF16)
    stores[0].start()
    stores[1].start()
    for store in stores:
        store.wait()


def back_kernel(meta, *refs):
    do_refs, refs = refs[:NY], refs[NY:]
    x_refs, refs = refs[:NY], refs[NY:]
    qkv_ref, lse_ref, a1_ref, w_ref, r0_ref, k_ref = refs[:6]
    dh_refs, refs = refs[6 : 6 + NY], refs[6 + NY :]
    gq_ref, doh, dq, dk, dv, dqkv, dh, gvec = refs
    y = meta[M_ZXY + 2]
    for k in range(NY):
        for j in range(SLOTS):
            rows = pl.ds(pl.multiple_of(meta[M_INV + k * SLOTS + j] * BLK, BLK), BLK)
            piece = do_refs[k][j * BLK : (j + 1) * BLK, :]
            for h in range(HEADS):
                doh[h, rows, :] = piece[:, h * HD : (h + 1) * HD]
    dk[...] = jnp.zeros_like(dk)
    dv[...] = jnp.zeros_like(dv)

    def head(h, carry):
        for tile in TILES:
            q0, k0, count = tile
            q = qkv_ref[h, q0 : q0 + 256, :]
            k = qkv_ref[HEADS + h, k0 : k0 + count, :]
            v = qkv_ref[2 * HEADS + h, k0 : k0 + count, :]
            do = doh[h, q0 : q0 + 256, :]
            scores = jnp.where(visible_mask(meta, tile), dot_nt(q, k) * SCALE, MASKED_SCORE)
            probs = jnp.exp(scores - lse_ref[h, q0 : q0 + 256, :])
            dp = dot_nt(do, v)
            row_dot = jnp.sum(dp * probs, axis=-1, keepdims=True)
            ds = (probs * (dp - row_dot)).astype(BF16)
            dq[h, q0 : q0 + 256, :] = dot_nn(ds, k) * SCALE
            dk[h, k0 : k0 + count, :] += dot_tn(ds, q)
            dv[h, k0 : k0 + count, :] += dot_tn(probs.astype(BF16), do)
        return carry

    lax.fori_loop(0, HEADS, head, 0)

    def join(t, carry):
        rows = pl.ds(pl.multiple_of(t * 256, 256), 256)
        parts = [dq[h, rows, :] for h in range(HEADS)]
        parts += [dk[h, rows, :] * SCALE for h in range(HEADS)]
        parts += [dv[h, rows, :] for h in range(HEADS)]
        joined = jnp.concatenate(parts, axis=1).astype(BF16)
        dqkv[rows, :] = joined
        dh[rows, :] = dot_nt(joined, w_ref[:, 0:WQ])
        return carry + jnp.sum(joined.astype(F32), axis=0, keepdims=True)

    sums = lax.fori_loop(0, GROWS // 256, join, jnp.zeros((1, WQ), F32))
    gain_sum = jnp.zeros((1, D), F32)
    shift_sum = jnp.zeros((1, D), F32)
    for k in range(NY):
        for j in range(SLOTS):
            rows = pl.ds(pl.multiple_of(meta[M_INV + k * SLOTS + j] * BLK, BLK), BLK)
            here = slice(j * BLK, (j + 1) * BLK)
            value = dh[rows, :]
            hat, _ = normed(x_refs[k][here, :].astype(F32))
            gain_sum += jnp.sum(value * hat, axis=0, keepdims=True)
            shift_sum += jnp.sum(value, axis=0, keepdims=True)
            dh_refs[k][here, :] = value.astype(dh_refs[k].dtype)
    gvec[...] = jnp.zeros_like(gvec)
    gvec[64:65, :] = gain_sum
    gvec[65:66, :] = shift_sum
    q_sum = sums[:, 0:HW]
    v_sum = sums[:, 2 * HW : 3 * HW]
    odd = k_ref[...] == 1
    for i in range(2):
        keep = odd if i else jnp.logical_not(odd)
        row = jnp.zeros((8, D), F32)
        for part, start in ((q_sum, 0), (v_sum, 384)):
            value = jnp.broadcast_to(jnp.where(keep, part, 0.0), (8, HW)).astype(BF16)
            row = row + dot_nt(value, select_matrix(r0_ref[...], start + 96 * y))
        gvec[66 + i : 67 + i, :] = row[0:1]

    def grads(c, carry):
        rows = pl.ds(pl.multiple_of(c * 256, 256), 256)
        gq_ref[rows, 0:WQ] = dot_tn(a1_ref[:, rows], dqkv[...]).astype(BF16)
        return carry

    lax.fori_loop(0, 3, grads, 0)
    gq_ref[:, WQ:QCOLS] = jnp.transpose(gvec[...])[:, 64:128].astype(BF16)


def end_kernel(*refs):
    dh_refs = refs[:NY]
    x_ref, dy_ref, gain_ref, out_ref = refs[NY:]
    dh = dh_refs[0][...]
    for k in range(1, NY):
        dh = dh + dh_refs[k][...].astype(F32)
    hat, scale = normed(x_ref[...].astype(F32))
    dhat = dh * gain_ref[0:1, :]
    mean_a = jnp.mean(dhat, axis=-1, keepdims=True)
    mean_b = jnp.mean(dhat * hat, axis=-1, keepdims=True)
    out_ref[...] = (dy_ref[...] + scale * (dhat - mean_a - hat * mean_b)).astype(BF16)


def params(mib):
    return pltpu.CompilerParams(vmem_limit_bytes=mib * 2**20)


VMEM = pl.BlockSpec(memory_space=pltpu.VMEM)
SMEM = pl.BlockSpec(memory_space=pltpu.SMEM)
ANY = pl.BlockSpec(memory_space=pl.ANY)


def cost(flops, nbytes):
    return pl.CostEstimate(flops=int(flops), bytes_accessed=int(nbytes), transcendentals=0)


def on_device(
    nz,
    nx,
    nc,
    tokens,
    slot_seq,
    slot_block_index,
    lengths,
    ln1_gain,
    ln1_bias,
    w_qkv,
    qv_bias,
    w_out,
    out_bias,
    ln2_gain,
    ln2_bias,
    w_fc,
    feed_input_bias,
    w_proj,
    proj_bias,
    cotangent,
):
    r6 = w_qkv.shape[0]
    r24 = NY * r6
    count = nz * nx * nc
    y = lax.axis_index("seq")
    f = lax.axis_index("fsdp")
    z, x, c = f // (nx * nc), (f // nc) % nx, f % nc

    def shift_y(value, k):
        return lax.ppermute(value, "seq", [(i, (i + k) % NY) for i in range(NY)])

    def shift_f(value, dz, dx, dc):
        pairs = []
        for i in range(count):
            iz, ix, ic = i // (nx * nc), (i // nc) % nx, i % nc
            to = (((iz + dz) % nz) * nx + (ix + dx) % nx) * nc + (ic + dc) % nc
            pairs.append((i, to))
        return lax.ppermute(value, "fsdp", pairs)

    def pick(value, i, axis=0):
        return lax.dynamic_index_in_dim(value, i, axis, keepdims=False)

    rel = np.arange(GSLOTS)
    absolute = ((y - rel // SLOTS) % NY) * SLOTS + rel % SLOTS
    chosen = absolute[:, None] == np.arange(GSLOTS)[None, :]
    seqs = jnp.sum(jnp.where(chosen, slot_seq[None, :], 0), axis=1)
    blocks = jnp.sum(jnp.where(chosen, slot_block_index[None, :], 0), axis=1)
    lens = jnp.sum(
        jnp.where(seqs[:, None] == np.arange(lengths.shape[1])[None, :], lengths[0:1, :], 0), axis=1
    )
    order = jnp.where(lens == LONG_LEN, 0, (seqs + 1) * 16) + blocks
    inverse = jnp.sum((order[None, :] < order[:, None]).astype(jnp.int32), axis=1)
    short = inverse[None, :] == (LONG + np.arange(4))[:, None]
    codes = jnp.sum(jnp.where(short, (seqs * SEQ_STRIDE + blocks * BLK)[None, :], 0), axis=1)
    bases = jnp.sum(jnp.where(short, (seqs * SEQ_STRIDE)[None, :], 0), axis=1)
    limits = jnp.sum(jnp.where(short, (seqs * SEQ_STRIDE + lens)[None, :], 0), axis=1)
    place = jnp.stack([z, x, y]).astype(jnp.int32)
    alive = (lens - blocks * BLK)[:SLOTS]
    meta = jnp.concatenate([inverse, codes, bases, limits, place, alive, jnp.zeros((2,), jnp.int32)])
    lane = np.arange(HW)
    r0 = jnp.asarray(((lane // (2 * r6)) * r6 + lane % r6)[None, :], jnp.int32)
    kk = jnp.asarray(((lane // r6) % 2)[None, :], jnp.int32)

    token_parts = [tokens] + [shift_y(tokens, k) for k in range(1, NY)]
    vec = jnp.concatenate(
        [
            ln1_gain[:, None],
            ln1_bias[:, None],
            qv_bias.reshape(2, r6).T,
            out_bias[:, None],
            ln2_gain[:, None],
            ln2_bias[:, None],
            proj_bias[:, None],
            feed_input_bias.reshape(r6, 4),
            jnp.zeros((r6, 116), BF16),
        ],
        axis=1,
    )
    fc_local = w_fc.reshape(r6, count, 4, r24).transpose(0, 2, 1, 3).reshape(r6, FF)
    payload = jnp.concatenate([w_qkv, w_out, fc_local, w_proj.reshape(r6, 4 * D), vec], axis=1)
    spread = lax.all_gather(payload, "seq", axis=0, tiled=False)
    v0 = 3 * D + D + 2 * FF
    vec_rows = spread[:, :, v0 : v0 + 8].reshape(r24, 8)
    qkv_mine = pick(spread[:, :, : 3 * D].reshape(r24, 3, NY, HW), y, 2).reshape(r24, WQ)
    wq_local = jnp.concatenate([qkv_mine, vec_rows, jnp.zeros((r24, 56), BF16)], axis=1)
    proj_rows = (
        spread[:, :, 4 * D + FF : v0].reshape(NY, r24, D).transpose(1, 0, 2).reshape(r24, NY * D)
    )
    fcb_rows = spread[:, :, v0 + 8 : v0 + 12].reshape(NY, r24).T
    w_local = jnp.concatenate(
        [
            spread[:, :, 3 * D : 4 * D + FF].reshape(r24, D + FF),
            proj_rows,
            vec_rows,
            fcb_rows,
            jnp.zeros((r24, 116), BF16),
        ],
        axis=1,
    )
    weights = lax.all_gather(w_local, "fsdp", axis=0, tiled=True)

    pair = wq_local
    if nc == 2:
        other = shift_f(wq_local, 0, 0, 1)
        first = jnp.where(c == 0, wq_local, other)
        second = jnp.where(c == 0, other, wq_local)
        pair = jnp.concatenate([first, second], axis=0)
    line = jnp.stack([pair] + [shift_f(pair, 0, k, 0) for k in range(1, nx)])
    planes = [line] + [shift_f(line, k, 0, 0) for k in range(1, nz)]

    front = pl.pallas_call(
        lambda *refs: front_kernel(nz, nx, *refs),
        in_specs=[SMEM] + [VMEM] * (NY + nz + 2),
        out_specs=[VMEM] * (5 + NY),
        out_shape=[
            jax.ShapeDtypeStruct((GROWS, D), BF16),
            jax.ShapeDtypeStruct((9, GROWS, HD), BF16),
            jax.ShapeDtypeStruct((HEADS, GROWS, 1), F32),
        ]
        + [jax.ShapeDtypeStruct((ROWS, HW), BF16)] * NY
        + [jax.ShapeDtypeStruct((D, QCOLS), BF16), jax.ShapeDtypeStruct((8, D), F32)],
        scratch_shapes=[pltpu.VMEM((HEADS, GROWS, HD), F32)],
        compiler_params=params(48),
        cost_estimate=cost(8e9, 15e6),
        name="front",
    )(meta, *token_parts, *planes, r0, kk)
    acts, qkv, lse = front[:3]
    mixed = front[3 : 3 + NY]
    wq, gain_one = front[3 + NY :]

    mixed_parts = [mixed[0]] + [shift_y(mixed[NY - k], k) for k in range(1, NY)]
    middle = pl.pallas_call(
        middle_kernel,
        in_specs=[SMEM] + [VMEM] * (NY + 2) + [ANY],
        out_specs=[VMEM] * (2 + NY) + [ANY],
        out_shape=[jax.ShapeDtypeStruct((ROWS, D), BF16), jax.ShapeDtypeStruct((ROWS, D), F32)]
        + [jax.ShapeDtypeStruct((ROWS, HW), BF16)] * NY
        + [jax.ShapeDtypeStruct((D, WCOLS), BF16)],
        scratch_shapes=[
            pltpu.VMEM((D, WCOLS), BF16),
            pltpu.VMEM((D, WCOLS), BF16),
            pltpu.VMEM((ROWS, D), F32),
            pltpu.VMEM((ROWS, D), F32),
            pltpu.VMEM((ROWS, 1), F32),
            pltpu.VMEM((ROWS, D), BF16),
            pltpu.VMEM((D, ROWS), BF16),
            pltpu.VMEM((ROWS, D), BF16),
            pltpu.VMEM((ROWS, D), F32),
            pltpu.VMEM((ROWS, D), F32),
            pltpu.VMEM((12, 8, 256), F32),
            pltpu.VMEM((128, D), F32),
            pltpu.SemaphoreType.DMA((8,)),
        ],
        compiler_params=params(52),
        cost_estimate=cost(13e9, 28e6),
        name="middle",
    )(meta, *mixed_parts, tokens, cotangent, weights)
    block_out, middle_grad = middle[:2]
    do_made = middle[2 : 2 + NY]
    reduced = lax.psum_scatter(middle[2 + NY], "fsdp", scatter_dimension=0, tiled=True)
    reduced = lax.optimization_barrier(reduced)

    do_parts = [do_made[0]] + [shift_y(do_made[NY - k], k) for k in range(1, NY)]
    back = pl.pallas_call(
        back_kernel,
        in_specs=[SMEM] + [VMEM] * (2 * NY + 6),
        out_specs=[VMEM] * (NY + 1),
        out_shape=[jax.ShapeDtypeStruct((ROWS, D), F32)]
        + [jax.ShapeDtypeStruct((ROWS, D), BF16)] * (NY - 1)
        + [jax.ShapeDtypeStruct((D, QCOLS), BF16)],
        scratch_shapes=[
            pltpu.VMEM((HEADS, GROWS, HD), BF16),
            pltpu.VMEM((HEADS, GROWS, HD), F32),
            pltpu.VMEM((HEADS, GROWS, HD), F32),
            pltpu.VMEM((HEADS, GROWS, HD), F32),
            pltpu.VMEM((GROWS, WQ), BF16),
            pltpu.VMEM((GROWS, D), F32),
            pltpu.VMEM((128, D), F32),
        ],
        compiler_params=params(56),
        cost_estimate=cost(12e9, 20e6),
        name="back",
    )(meta, *do_parts, *token_parts, qkv, lse, acts, wq, r0, kk)
    dh_made = back[:NY]
    dh_parts = [dh_made[0]] + [shift_y(dh_made[NY - k], k) for k in range(1, NY)]
    tokens_grad = pl.pallas_call(
        end_kernel,
        in_specs=[VMEM] * (NY + 3),
        out_specs=VMEM,
        out_shape=jax.ShapeDtypeStruct((ROWS, D), BF16),
        compiler_params=params(24),
        cost_estimate=cost(1e7, 6e6),
        name="end",
    )(*dh_parts, tokens, middle_grad, gain_one)

    def exchange(value, i, n, send):
        total = pick(value, i).astype(F32)
        for k in range(1, n):
            total = total + send(pick(value, (i + k) % n), k).astype(F32)
        return total.astype(BF16)

    gq = back[NY].reshape(nz, nx, nc, r24, QCOLS)
    if nc == 2:
        kept = pick(gq, c, 2).astype(F32)
        gq = (kept + shift_f(pick(gq, 1 - c, 2), 0, 0, 1).astype(F32)).astype(BF16)
    else:
        gq = gq[:, :, 0]
    gq = exchange(gq, z, nz, lambda v, k: shift_f(v, k, 0, 0))
    gq = exchange(gq, x, nx, lambda v, k: shift_f(v, 0, k, 0))

    row_part = jnp.concatenate(
        [reduced[:, :C_PROJ], reduced[:, C_VEC : C_VEC + 8], gq[:, WQ : WQ + 8], gq[:, :WQ]], axis=1
    ).reshape(NY, r6, C_PROJ + 16 + WQ)
    proj_part = jnp.concatenate([reduced[:, C_PROJ:C_VEC].reshape(r24, NY, D)], axis=0)
    proj_part = jnp.transpose(proj_part, (1, 0, 2))
    fcb_part = jnp.pad(reduced[:, C_VEC + 8 : C_VEC + 12].T[:, :, None], ((0, 0), (0, 0), (0, 127)))
    proj_part = jnp.concatenate([proj_part, fcb_part], axis=2)
    row_parts = [pick(row_part, y)]
    proj_parts = [pick(proj_part, y)]
    for k in range(1, NY):
        row_parts.append(shift_y(pick(row_part, (y + k) % NY), k))
        proj_parts.append(shift_y(pick(proj_part, (y + k) % NY), k))
    rows_sum = sum(part[:, : C_PROJ + 16].astype(F32) for part in row_parts)
    proj_sum = sum(part.astype(F32) for part in proj_parts)
    heads = jnp.stack([part[:, C_PROJ + 16 :] for part in row_parts])
    heads = jnp.concatenate([pick(heads, (y - q) % NY)[:, None] for q in range(NY)], axis=1)
    grad_qkv = heads.reshape(r6, NY, 3, HW).transpose(0, 2, 1, 3).reshape(r6, 3 * D).astype(F32)
    grad_fc = rows_sum[:, C_FC:C_PROJ].reshape(r6, NY, count, r24).transpose(0, 2, 1, 3)
    vecs = rows_sum[:, C_PROJ:]
    return (
        block_out,
        tokens_grad,
        vecs[:, 8],
        vecs[:, 9],
        grad_qkv,
        vecs[:, 10:12].T.reshape(2 * r6),
        rows_sum[:, :D],
        vecs[:, 4],
        vecs[:, 5],
        vecs[:, 6],
        grad_fc.reshape(r6, FF),
        proj_sum[:, D],
        proj_sum[:, :D],
        vecs[:, 7],
    )


def solution(mesh):
    both = P(("fsdp", "seq"))
    wide = P(("fsdp", "seq"), None)
    nz, nx, nc = (4, 4, 2) if mesh.shape["fsdp"] == 32 else (1, 1, mesh.shape["fsdp"])
    in_specs = (wide, P("fsdp"), P("fsdp"), P("fsdp", None), both, both, wide, both, wide)
    in_specs += (both, both, both, wide, both, wide, both, wide)
    out_specs = (wide, wide, both, both, wide, both, wide, both, both, both, wide, both, wide, both)

    def program(*args):
        return on_device(nz, nx, nc, *args)

    return jax.shard_map(
        program, mesh=mesh, in_specs=in_specs, out_specs=out_specs, check_vma=False
    )
```

```python
import numpy as np
import jax
import jax.numpy as jnp
from jax import lax
from jax.experimental import pallas as pl
from jax.experimental.pallas import tpu as pltpu
from jax.sharding import PartitionSpec as P

D = 768
H = 12
HD = 64
FF = 3072
BLK = 128
SLOTS = 3
NY = 4
GSLOTS = SLOTS * NY
ROWS = SLOTS * BLK
GROWS = GSLOTS * BLK
LONG = 8
LONG_LEN = LONG * BLK
HEADS = H // NY
HW = HEADS * HD
WQ = 3 * HW
QCOLS = 640
C_FC = 768
C_PROJ = C_FC + FF
C_VEC = C_PROJ + FF
WCOLS = C_VEC + 128
EPSILON = 1e-05
MASKED_SCORE = -1e30
SCALE = HD**-0.5
SEQ_STRIDE = 4096
M_INV, M_CODE, M_BASE, M_LIM, M_ZXY, M_THR, M_CORE = 0, 12, 16, 20, 24, 27, 30
F32 = jnp.float32
BF16 = jnp.bfloat16
TILES = tuple((256 * t, 0, 256 * (t + 1)) for t in range(4)) + ((1024, 1024, 256), (1280, 1024, 512))


def dot_nn(a, b):
    return lax.dot_general(a, b, (((1,), (0,)), ((), ())), preferred_element_type=F32)


def dot_nt(a, b):
    return lax.dot_general(a, b, (((1,), (1,)), ((), ())), preferred_element_type=F32)


def dot_tn(a, b):
    return lax.dot_general(a, b, (((0,), (0,)), ((), ())), preferred_element_type=F32)


def normed(value):
    center = jnp.mean(value, axis=-1, keepdims=True)
    offset = value - center
    spread = jnp.mean(offset * offset, axis=-1, keepdims=True)
    scale = lax.rsqrt(spread + EPSILON)
    return offset * scale, scale


def minus(a, k, n):
    r = a - k
    return jnp.where(r < 0, r + n, r)


def visible_mask(meta, tile):
    q0, k0, count = tile
    row = lax.broadcasted_iota(jnp.int32, (256, 1), 0)
    col = lax.broadcasted_iota(jnp.int32, (1, count), 1)
    if q0 < LONG_LEN:
        return col <= row + q0
    first = (q0 - LONG_LEN) // BLK

    def per_slot(base, index, start, n):
        value = jnp.full(index.shape, meta[base + start], jnp.int32)
        for i in range(1, n):
            value = jnp.where(index >= i * BLK, meta[base + start + i], value)
        return value

    q_code = per_slot(M_CODE, row, first, 2) + (row & (BLK - 1))
    q_base = per_slot(M_BASE, row, first, 2)
    slots = count // BLK
    k_code = per_slot(M_CODE, col, 0, slots) + (col & (BLK - 1))
    k_lim = per_slot(M_LIM, col, 0, slots)
    k_code = jnp.where(k_code < k_lim, k_code, 1 << 24)
    return (k_code <= q_code) & (k_code >= q_base)


def select_matrix(r0, offset):
    rows = lax.broadcasted_iota(jnp.int32, (D, HW), 0)
    return jnp.where(rows == r0 + offset, 1.0, 0.0).astype(BF16)


def front_kernel(nz, nx, meta, *refs):
    x_refs, refs = refs[:NY], refs[NY:]
    z_refs, refs = refs[:nz], refs[nz:]
    r0_ref, k_ref = refs[:2]
    a1_ref, qkv_ref, lse_ref = refs[2:5]
    o_refs = refs[5 : 5 + NY]
    w_ref, gain_ref, oh = refs[5 + NY :]
    z, x, y = meta[M_ZXY], meta[M_ZXY + 1], meta[M_ZXY + 2]
    step = D // (nz * nx)
    for kz in range(nz):
        for kx in range(nx):
            at = (minus(z, kz, nz) * nx + minus(x, kx, nx)) * step
            w_ref[pl.ds(pl.multiple_of(at, step), step), :] = z_refs[kz][kx]
    vectors = jnp.transpose(w_ref[:, 512:640].astype(F32))
    gain = vectors[64:65]
    shift = vectors[65:66]
    gain_ref[...] = jnp.broadcast_to(gain, (8, D))
    small = vectors[64:72].astype(BF16)
    odd = k_ref[...] == 1
    sums = dot_nn(small, select_matrix(r0_ref[...], 96 * y))
    q_bias = jnp.where(odd, sums[3:4], sums[2:3])
    sums = dot_nn(small, select_matrix(r0_ref[...], 384 + 96 * y))
    v_bias = jnp.where(odd, sums[3:4], sums[2:3])
    bias = jnp.concatenate([q_bias, jnp.zeros((1, HW), F32), v_bias], axis=1)
    for k in range(NY):
        for j in range(SLOTS):
            hat, _ = normed(x_refs[k][j * BLK : (j + 1) * BLK, :].astype(F32))
            to = pl.multiple_of(meta[M_INV + k * SLOTS + j] * BLK, BLK)
            a1_ref[pl.ds(to, BLK), :] = (hat * gain + shift).astype(BF16)

    def project(t, carry):
        rows = pl.ds(pl.multiple_of(t * 256, 256), 256)
        joined = (dot_nn(a1_ref[rows, :], w_ref[:, 0:WQ]) + bias).astype(BF16)
        for i in range(9):
            qkv_ref[i, rows, :] = joined[:, i * HD : (i + 1) * HD]
        return carry

    lax.fori_loop(0, GROWS // 256, project, 0)

    def head(h, carry):
        for tile in TILES:
            q0, k0, count = tile
            q = qkv_ref[h, q0 : q0 + 256, :]
            k = qkv_ref[HEADS + h, k0 : k0 + count, :]
            v = qkv_ref[2 * HEADS + h, k0 : k0 + count, :]
            scores = jnp.where(visible_mask(meta, tile), dot_nt(q, k) * SCALE, MASKED_SCORE)
            top = jnp.max(scores, axis=-1, keepdims=True)
            weights = jnp.exp(scores - top)
            total = jnp.sum(weights, axis=-1, keepdims=True)
            probs = (weights * (1.0 / total)).astype(BF16)
            oh[h, q0 : q0 + 256, :] = dot_nn(probs, v)
            lse_ref[h, q0 : q0 + 256, :] = top + jnp.log(total)
        return carry

    lax.fori_loop(0, HEADS, head, 0)
    for k in range(NY):
        for j in range(SLOTS):
            rows = pl.ds(pl.multiple_of(meta[M_INV + k * SLOTS + j] * BLK, BLK), BLK)
            mixed = jnp.concatenate([oh[h, rows, :] for h in range(HEADS)], axis=1)
            o_refs[k][j * BLK : (j + 1) * BLK, :] = mixed.astype(BF16)


GELU_C = float(np.sqrt(2.0 / np.pi))


def hidden_step(q, w, bias, a2, a2t, dz, acc, acc_da, g):
    at_fc = slice(q * D, (q + 1) * D)
    at_p = slice((4 + q) * D, (5 + q) * D)
    u = dot_nn(a2[...], w[:, at_fc]) + bias
    t = jnp.tanh(GELU_C * (u + 0.044715 * (u * u * u)))
    m = (0.5 * u * (1.0 + t)).astype(BF16)
    slope = 0.5 * (1.0 + t) + (0.5 * GELU_C) * u * (1.0 - t * t) * (1.0 + 0.134145 * (u * u))
    du = (dot_nt(dz[...], w[:, at_p]) * slope).astype(BF16)
    g[:, at_p] = dot_tn(m, dz[...]).astype(BF16)
    g[:, at_fc] = dot_nn(a2t[...], du).astype(BF16)
    acc[...] += dot_nn(m, w[:, at_p])
    acc_da[...] += dot_nt(du, w[:, at_fc])
    return jnp.sum(du.astype(F32), axis=0, keepdims=True)


def middle_kernel(meta, *refs):
    o_refs, refs = refs[:NY], refs[NY:]
    x_ref, cot_ref, w_hbm = refs[:3]
    out_ref, dy_ref = refs[3:5]
    do_refs, refs = refs[5 : 5 + NY], refs[5 + NY :]
    rest, g_hbm, w, g, gw, hat2, dz, a2, a2t, acc, acc_da, gvec, sems = refs
    y = meta[M_ZXY + 2]
    spans = [(0, 8 * D, D), (C_VEC, 9 * D, 128)]
    for q in range(4):
        spans += [(C_FC + q * D, q * D, D), (C_PROJ + q * D, (4 + q) * D, D)]
    loads = [
        pltpu.make_async_copy(w_hbm.at[:, pl.ds(a, n)], w.at[:, pl.ds(b, n)], sems.at[i])
        for i, (a, b, n) in enumerate(spans)
    ]
    stores = [
        pltpu.make_async_copy(
            g.at[:, pl.ds(i * D, D)], g_hbm.at[:, pl.ds(i * D, D)], sems.at[10 + i]
        )
        for i in range(8)
    ]
    for load in loads:
        load.start()
    offset = lax.broadcasted_iota(jnp.int32, (BLK, 1), 0)
    for j in range(SLOTS):
        rows = slice(j * BLK, (j + 1) * BLK)
        live = jnp.where(offset < meta[M_THR + j], 1.0, 0.0)
        dz[rows, :] = (cot_ref[rows, :].astype(F32) * live).astype(BF16)
    loads[0].wait()
    loads[1].wait()
    vec = jnp.transpose(w[:, 9 * D : 9 * D + 128].astype(F32))
    total = x_ref[...].astype(F32) + vec[4:5, :]
    for k in range(NY):
        at = pl.ds(pl.multiple_of(minus(y, k, NY) * HW, HW), HW)
        total = total + dot_nn(o_refs[k][...], w[at, 8 * D : 9 * D])
    hat, scale = normed(total)
    hat2[...] = hat
    acts = hat * vec[5:6, :] + vec[6:7, :]
    a2[...] = acts.astype(BF16)
    a2t[...] = jnp.transpose(acts).astype(BF16)
    acc[...] = total + vec[7:8, :]
    acc_da[...] = jnp.zeros_like(acc_da)
    gvec[...] = jnp.zeros_like(gvec)
    for q in range(4):
        loads[2 + 2 * q].wait()
        loads[3 + 2 * q].wait()
        row = hidden_step(q, w, vec[8 + q : 9 + q, :], a2, a2t, dz, acc, acc_da, g)
        gvec[8 + q : 9 + q, :] = row
        stores[q].start()
        stores[4 + q].start()
    out_ref[...] = acc[...].astype(BF16)
    da2 = acc_da[...]
    hat = hat2[...]
    gvec[6:7, :] = jnp.sum(da2, axis=0, keepdims=True)
    gvec[5:6, :] = jnp.sum(da2 * hat, axis=0, keepdims=True)
    dhat = da2 * vec[5:6, :]
    mean_a = jnp.mean(dhat, axis=-1, keepdims=True)
    mean_b = jnp.mean(dhat * hat, axis=-1, keepdims=True)
    dz32 = dz[...].astype(F32)
    dy = dz32 + scale * (dhat - mean_a - hat * mean_b)
    dy_ref[...] = dy
    da = dy.astype(BF16)
    gvec[7:8, :] = jnp.sum(dz32, axis=0, keepdims=True)
    gvec[4:5, :] = jnp.sum(da.astype(F32), axis=0, keepdims=True)
    for k in range(NY):
        at = pl.ds(pl.multiple_of(minus(y, k, NY) * HW, HW), HW)
        do_refs[k][...] = dot_nt(da, w[at, 8 * D : 9 * D]).astype(BF16)
        gw[at, :] = dot_tn(o_refs[k][...], da)
    rest[:, 0:D] = gw[...].astype(BF16)
    rest[:, D : D + 128] = jnp.transpose(gvec[...]).astype(BF16)
    for store in stores:
        store.wait()


def hidden_order(count, r24):
    return [
        (d * 4 * r24 + q * r24, (q * count + d) * r24) for q in range(NY) for d in range(count)
    ]


def pack_kernel(count, r6, *refs):
    sources, out, wide, vec = refs[:12], refs[12], refs[13], refs[14]
    local, sems = refs[15:27], refs[27]
    loads = [
        pltpu.make_async_copy(source, local[i], sems.at[i]) for i, source in enumerate(sources)
    ]
    for load in loads:
        load.start()
    r24 = NY * r6
    rows = out.shape[0]
    out[...] = jnp.zeros_like(out)
    vec[...] = jnp.zeros_like(vec)
    for load in loads:
        load.wait()
    wq, wo, wf, wp, g1, b1, qv, ob, g2, b2, fb, pb = local
    out[0:r6, 0 : 3 * D] = wq[...]
    out[0:r6, 3 * D : 4 * D] = wo[...]
    value = wf[...].astype(F32)
    for natural, packed in hidden_order(count, r24):
        wide[:, packed : packed + r24] = value[:, natural : natural + r24]
    out[0:r6, 4 * D : 4 * D + FF] = wide[...].astype(BF16)
    value = wp[...].astype(F32)
    for i in range(r24 // rows):
        at = 4 * D + FF + i * D
        out[:, at : at + D] = value[i * rows : (i + 1) * rows, :].astype(BF16)
    vec[0:1, 0:r6] = g1[...].astype(F32)
    vec[1:2, 0:r6] = b1[...].astype(F32)
    both = qv[...].astype(F32)
    vec[2:3, 0:r6] = both[:, 0:r6]
    vec[3:4, 0:r6] = both[:, r6 : 2 * r6]
    vec[4:5, 0:r6] = ob[...].astype(F32)
    vec[5:6, 0:r6] = g2[...].astype(F32)
    vec[6:7, 0:r6] = b2[...].astype(F32)
    vec[7:8, 0:r6] = pb[...].astype(F32)
    hidden = fb[...].astype(F32)
    for i in range(r24 // rows):
        vec[8 + i : 9 + i, 0:rows] = hidden[:, i * rows : (i + 1) * rows]
    at = out.shape[1] - 128
    out[:, at : at + 128] = jnp.transpose(vec[...])[0:rows, :].astype(BF16)


def turns_kernel(n, base, meta, *refs):
    parts, outs, total = refs[: -n - 1], refs[-n - 1 : -1], refs[-1]
    value = parts[0][...].astype(F32)
    for part in parts[1:]:
        value = value + part[...].astype(F32)
    total[...] = value
    size = total.shape[0] // n
    for k in range(n):
        at = lax.rem(meta[base] + k, n) * size
        outs[k][...] = total[pl.ds(at, size)].astype(BF16)


def rows_kernel(n, r6, meta, *refs):
    parts, outs = refs[:n], refs[n:]
    total = parts[0][...].astype(F32)
    for part in parts[1:]:
        total = total + part[...].astype(F32)
    y = meta[M_ZXY + 2]
    r24, width = total.shape
    rows = outs[0].shape[0]
    i = lax.broadcasted_iota(jnp.int32, (rows, r24), 0)
    j = lax.broadcasted_iota(jnp.int32, (rows, r24), 1)
    lane = lax.broadcasted_iota(jnp.int32, (rows, 128), 1)
    value = total.astype(BF16)
    bias = value[:, D : D + 128]
    for k in range(NY):
        to = lax.rem(y + k, NY)
        chosen = jnp.where((i < r6) & (j == i + to * r6), 1.0, 0.0).astype(BF16)
        outs[k][:, 0:width] = dot_nn(chosen, value).astype(BF16)
        hidden = jnp.zeros((rows, 128), F32)
        for g in range(r24 // rows):
            group = dot_nn(jnp.where(j == i + g * rows, 1.0, 0.0).astype(BF16), bias)
            column = jnp.sum(jnp.where(lane == 8 + to, group, 0.0), axis=1, keepdims=True)
            hidden = hidden + jnp.where(lane == g, column, 0.0)
        outs[k][:, width : width + 128] = hidden.astype(BF16)


def split_kernel(r6, meta, reduced, *refs):
    outs, (blocks,) = refs[:NY], refs[NY:]
    r24 = NY * r6
    rows = outs[0].shape[0]
    y = meta[M_ZXY + 2]
    for q in range(NY):
        blocks[q] = reduced[:, FF + q * D : FF + (q + 1) * D].astype(F32)
    i = lax.broadcasted_iota(jnp.int32, (rows, r24), 0)
    j = lax.broadcasted_iota(jnp.int32, (rows, r24), 1)
    for k in range(NY):
        to = lax.rem(y + k, NY)
        chosen = jnp.where((i < r6) & (j == i + to * r6), 1.0, 0.0).astype(BF16)
        outs[k][:, 0:FF] = dot_nn(chosen, reduced[:, 0:FF]).astype(BF16)
        value = blocks[to]
        for n in range(r24 // rows):
            outs[k][:, FF + n * D : FF + (n + 1) * D] = value[n * rows : (n + 1) * rows, :].astype(
                BF16
            )


def join_kernel(count, r6, *refs):
    parts, (fc, proj) = refs[:NY], refs[NY:]
    r24 = NY * r6
    rows = parts[0].shape[0]
    total = parts[0][...].astype(F32)
    for k in range(1, NY):
        total = total + parts[k][...].astype(F32)
    for natural, packed in hidden_order(count, r24):
        fc[:, natural : natural + r24] = total[0:r6, packed : packed + r24]
    for n in range(r24 // rows):
        proj[n * rows : (n + 1) * rows, :] = total[:, FF + n * D : FF + (n + 1) * D]


def back_kernel(nc, meta, *refs):
    do_refs, refs = refs[:NY], refs[NY:]
    x_refs, refs = refs[:NY], refs[NY:]
    qkv_ref, lse_ref, a1_ref, w_ref, r0_ref, k_ref, rest = refs[:7]
    dh_refs, refs = refs[7 : 7 + NY], refs[7 + NY :]
    halves, refs = refs[:nc], refs[nc:]
    doh, dq, dk, dv, dqkv, dh, gvec, gq_ref = refs
    y = meta[M_ZXY + 2]
    for k in range(NY):
        for j in range(SLOTS):
            rows = pl.ds(pl.multiple_of(meta[M_INV + k * SLOTS + j] * BLK, BLK), BLK)
            piece = do_refs[k][j * BLK : (j + 1) * BLK, :]
            for h in range(HEADS):
                doh[h, rows, :] = piece[:, h * HD : (h + 1) * HD]
    dk[...] = jnp.zeros_like(dk)
    dv[...] = jnp.zeros_like(dv)

    def head(h, carry):
        for tile in TILES:
            q0, k0, count = tile
            q = qkv_ref[h, q0 : q0 + 256, :]
            k = qkv_ref[HEADS + h, k0 : k0 + count, :]
            v = qkv_ref[2 * HEADS + h, k0 : k0 + count, :]
            do = doh[h, q0 : q0 + 256, :]
            scores = jnp.where(visible_mask(meta, tile), dot_nt(q, k) * SCALE, MASKED_SCORE)
            probs = jnp.exp(scores - lse_ref[h, q0 : q0 + 256, :])
            dp = dot_nt(do, v)
            row_dot = jnp.sum(dp * probs, axis=-1, keepdims=True)
            ds = (probs * (dp - row_dot)).astype(BF16)
            dq[h, q0 : q0 + 256, :] = dot_nn(ds, k) * SCALE
            dk[h, k0 : k0 + count, :] += dot_tn(ds, q)
            dv[h, k0 : k0 + count, :] += dot_tn(probs.astype(BF16), do)
        return carry

    lax.fori_loop(0, HEADS, head, 0)

    def join(t, carry):
        rows = pl.ds(pl.multiple_of(t * 256, 256), 256)
        parts = [dq[h, rows, :] for h in range(HEADS)]
        parts += [dk[h, rows, :] * SCALE for h in range(HEADS)]
        parts += [dv[h, rows, :] for h in range(HEADS)]
        joined = jnp.concatenate(parts, axis=1).astype(BF16)
        dqkv[rows, :] = joined
        dh[rows, :] = dot_nt(joined, w_ref[:, 0:WQ])
        return carry + jnp.sum(joined.astype(F32), axis=0, keepdims=True)

    sums = lax.fori_loop(0, GROWS // 256, join, jnp.zeros((1, WQ), F32))
    gain_sum = jnp.zeros((1, D), F32)
    shift_sum = jnp.zeros((1, D), F32)
    for k in range(NY):
        for j in range(SLOTS):
            rows = pl.ds(pl.multiple_of(meta[M_INV + k * SLOTS + j] * BLK, BLK), BLK)
            here = slice(j * BLK, (j + 1) * BLK)
            value = dh[rows, :]
            hat, _ = normed(x_refs[k][here, :].astype(F32))
            gain_sum += jnp.sum(value * hat, axis=0, keepdims=True)
            shift_sum += jnp.sum(value, axis=0, keepdims=True)
            dh_refs[k][here, :] = value.astype(dh_refs[k].dtype)
    gvec[...] = jnp.zeros_like(gvec)
    gvec[64:65, :] = gain_sum
    gvec[65:66, :] = shift_sum
    q_sum = sums[:, 0:HW]
    v_sum = sums[:, 2 * HW : 3 * HW]
    odd = k_ref[...] == 1
    for i in range(2):
        keep = odd if i else jnp.logical_not(odd)
        row = jnp.zeros((8, D), F32)
        for part, start in ((q_sum, 0), (v_sum, 384)):
            value = jnp.broadcast_to(jnp.where(keep, part, 0.0), (8, HW)).astype(BF16)
            row = row + dot_nt(value, select_matrix(r0_ref[...], start + 96 * y))
        gvec[66 + i : 67 + i, :] = row[0:1]

    def grads(c, carry):
        rows = pl.ds(pl.multiple_of(c * 256, 256), 256)
        gq_ref[rows, D + 128 : D + 128 + WQ] = dot_tn(a1_ref[:, rows], dqkv[...])
        return carry

    lax.fori_loop(0, 3, grads, 0)
    gq_ref[:, 0 : D + 128] = rest[...].astype(F32)
    gq_ref[:, D + 128 + WQ :] = jnp.transpose(gvec[...])[:, 64:128]
    blocks, size = halves[0].shape[:2]
    for k in range(nc):
        core = lax.rem(meta[M_CORE] + k, nc) * size
        for i in range(blocks):
            at = pl.multiple_of(i * size * nc + core, 8)
            halves[k][i] = gq_ref[pl.ds(at, size), :].astype(BF16)


def end_kernel(*refs):
    dh_refs = refs[:NY]
    x_ref, dy_ref, gain_ref, out_ref = refs[NY:]
    dh = dh_refs[0][...]
    for k in range(1, NY):
        dh = dh + dh_refs[k][...].astype(F32)
    hat, scale = normed(x_ref[...].astype(F32))
    dhat = dh * gain_ref[0:1, :]
    mean_a = jnp.mean(dhat, axis=-1, keepdims=True)
    mean_b = jnp.mean(dhat * hat, axis=-1, keepdims=True)
    out_ref[...] = (dy_ref[...] + scale * (dhat - mean_a - hat * mean_b)).astype(BF16)


def params(mib):
    return pltpu.CompilerParams(vmem_limit_bytes=mib * 2**20)


VMEM = pl.BlockSpec(memory_space=pltpu.VMEM)
SMEM = pl.BlockSpec(memory_space=pltpu.SMEM)
HBM = pl.BlockSpec(memory_space=pltpu.HBM)


def cost(flops, nbytes):
    return pl.CostEstimate(flops=int(flops), bytes_accessed=int(nbytes), transcendentals=0)


def on_device(
    nz,
    nx,
    nc,
    tokens,
    slot_seq,
    slot_block_index,
    lengths,
    ln1_gain,
    ln1_bias,
    w_qkv,
    qv_bias,
    w_out,
    out_bias,
    ln2_gain,
    ln2_bias,
    w_fc,
    feed_input_bias,
    w_proj,
    proj_bias,
    cotangent,
):
    r6 = w_qkv.shape[0]
    r24 = NY * r6
    count = nz * nx * nc
    y = lax.axis_index("seq")
    f = lax.axis_index("fsdp")
    z, x, c = f // (nx * nc), (f // nc) % nx, f % nc

    def shift_y(value, k):
        return lax.ppermute(value, "seq", [(i, (i + k) % NY) for i in range(NY)])

    def shift_f(value, dz, dx, dc):
        pairs = []
        for i in range(count):
            iz, ix, ic = i // (nx * nc), (i // nc) % nx, i % nc
            to = (((iz + dz) % nz) * nx + (ix + dx) % nx) * nc + (ic + dc) % nc
            pairs.append((i, to))
        return lax.ppermute(value, "fsdp", pairs)

    def pick(value, i, axis=0):
        return lax.dynamic_index_in_dim(value, i, axis, keepdims=False)

    rel = np.arange(GSLOTS)
    absolute = ((y - rel // SLOTS) % NY) * SLOTS + rel % SLOTS
    chosen = absolute[:, None] == np.arange(GSLOTS)[None, :]
    seqs = jnp.sum(jnp.where(chosen, slot_seq[None, :], 0), axis=1)
    blocks = jnp.sum(jnp.where(chosen, slot_block_index[None, :], 0), axis=1)
    lens = jnp.sum(
        jnp.where(seqs[:, None] == np.arange(lengths.shape[1])[None, :], lengths[0:1, :], 0), axis=1
    )
    order = jnp.where(lens == LONG_LEN, 0, (seqs + 1) * 16) + blocks
    inverse = jnp.sum((order[None, :] < order[:, None]).astype(jnp.int32), axis=1)
    short = inverse[None, :] == (LONG + np.arange(4))[:, None]
    codes = jnp.sum(jnp.where(short, (seqs * SEQ_STRIDE + blocks * BLK)[None, :], 0), axis=1)
    bases = jnp.sum(jnp.where(short, (seqs * SEQ_STRIDE)[None, :], 0), axis=1)
    limits = jnp.sum(jnp.where(short, (seqs * SEQ_STRIDE + lens)[None, :], 0), axis=1)
    place = jnp.stack([z, x, y]).astype(jnp.int32)
    alive = (lens - blocks * BLK)[:SLOTS]
    core = jnp.stack([c, jnp.zeros_like(c)]).astype(jnp.int32)
    meta = jnp.concatenate([inverse, codes, bases, limits, place, alive, core])
    lane = np.arange(HW)
    r0 = jnp.asarray(((lane // (2 * r6)) * r6 + lane % r6)[None, :], jnp.int32)
    kk = jnp.asarray(((lane // r6) % 2)[None, :], jnp.int32)

    rows8 = (r6 + 7) // 8 * 8
    groups = r24 // rows8
    width = 4 * D + FF + groups * D + 128
    vectors = (ln1_gain, ln1_bias, qv_bias, out_bias, ln2_gain, ln2_bias, feed_input_bias, proj_bias)
    sources = [w_qkv, w_out, w_fc, w_proj] + [v[None, :] for v in vectors]
    payload = pl.pallas_call(
        lambda *refs: pack_kernel(count, r6, *refs),
        in_specs=[HBM] * 12,
        out_specs=VMEM,
        out_shape=jax.ShapeDtypeStruct((rows8, width), BF16),
        scratch_shapes=[pltpu.VMEM((r6, FF), F32), pltpu.VMEM((128, max(128, rows8)), F32)]
        + [pltpu.VMEM(v.shape, BF16) for v in sources]
        + [pltpu.SemaphoreType.DMA((12,))],
        compiler_params=params(60),
        name="pack",
    )(*sources)
    payloads = [payload] + [shift_y(payload, k) for k in range(1, NY)]
    later, _ = lax.optimization_barrier((tokens, payload))
    token_parts = [tokens] + [shift_y(later, k) for k in range(1, NY)]
    spread = jnp.stack(payloads)
    spread = jnp.concatenate([pick(spread, (y - q) % NY)[None] for q in range(NY)])
    v0 = width - 128
    vec_rows = spread[:, :r6, v0 : v0 + 8].reshape(r24, 8)
    qkv_mine = pick(spread[:, :r6, : 3 * D].reshape(r24, 3, NY, HW), y, 2).reshape(r24, WQ)
    wq_local = jnp.concatenate([qkv_mine, vec_rows, jnp.zeros((r24, 56), BF16)], axis=1)
    proj_rows = jnp.concatenate(
        [
            jnp.concatenate(
                [
                    spread[q, :, 4 * D + FF + n * D : 4 * D + FF + (n + 1) * D]
                    for n in range(groups)
                ],
                axis=0,
            )
            for q in range(NY)
        ],
        axis=1,
    )
    fcb_rows = jnp.transpose(spread[:, :, v0 + 8 : v0 + 8 + groups], (2, 1, 0)).reshape(r24, NY)
    w_local = jnp.concatenate(
        [
            spread[:, :r6, 3 * D : 4 * D + FF].reshape(r24, D + FF),
            proj_rows,
            vec_rows,
            fcb_rows,
            jnp.zeros((r24, 116), BF16),
        ],
        axis=1,
    )
    weights = lax.all_gather(w_local, "fsdp", axis=0, tiled=True)

    pair = wq_local
    if nc == 2:
        other = shift_f(wq_local, 0, 0, 1)
        first = jnp.where(c == 0, wq_local, other)
        second = jnp.where(c == 0, other, wq_local)
        pair = jnp.concatenate([first, second], axis=0)
    line = jnp.stack([pair] + [shift_f(pair, 0, k, 0) for k in range(1, nx)])
    planes = [line] + [shift_f(line, k, 0, 0) for k in range(1, nz)]

    front = pl.pallas_call(
        lambda *refs: front_kernel(nz, nx, *refs),
        in_specs=[SMEM] + [VMEM] * (NY + nz + 2),
        out_specs=[VMEM] * (5 + NY),
        out_shape=[
            jax.ShapeDtypeStruct((GROWS, D), BF16),
            jax.ShapeDtypeStruct((9, GROWS, HD), BF16),
            jax.ShapeDtypeStruct((HEADS, GROWS, 1), F32),
        ]
        + [jax.ShapeDtypeStruct((ROWS, HW), BF16)] * NY
        + [jax.ShapeDtypeStruct((D, QCOLS), BF16), jax.ShapeDtypeStruct((8, D), F32)],
        scratch_shapes=[pltpu.VMEM((HEADS, GROWS, HD), F32)],
        compiler_params=params(60),
        cost_estimate=cost(8e9, 15e6),
        name="front",
    )(meta, *token_parts, *planes, r0, kk)
    acts, qkv, lse = front[:3]
    mixed = front[3 : 3 + NY]
    wq, gain_one = front[3 + NY :]

    mixed_parts = [mixed[0]] + [shift_y(mixed[NY - k], k) for k in range(1, NY)]
    wide32 = jax.ShapeDtypeStruct((ROWS, D), F32)
    wide16 = jax.ShapeDtypeStruct((ROWS, D), BF16)
    middle = pl.pallas_call(
        middle_kernel,
        in_specs=[SMEM] + [VMEM] * (NY + 2) + [HBM],
        out_specs=[VMEM] * (3 + NY) + [HBM],
        out_shape=[wide16, wide32]
        + [jax.ShapeDtypeStruct((ROWS, HW), BF16)] * NY
        + [
            jax.ShapeDtypeStruct((D, D + 128), BF16),
            jax.ShapeDtypeStruct((D, 8 * D), BF16),
        ],
        scratch_shapes=[
            pltpu.VMEM((D, 9 * D + 128), BF16),
            pltpu.VMEM((D, 8 * D), BF16),
            pltpu.VMEM((D, D), F32),
            pltpu.VMEM((ROWS, D), F32),
            pltpu.VMEM((ROWS, D), BF16),
            pltpu.VMEM((ROWS, D), BF16),
            pltpu.VMEM((D, ROWS), BF16),
            pltpu.VMEM((ROWS, D), F32),
            pltpu.VMEM((ROWS, D), F32),
            pltpu.VMEM((128, D), F32),
            pltpu.SemaphoreType.DMA((18,)),
        ],
        compiler_params=params(60),
        cost_estimate=cost(13e9, 28e6),
        name="middle",
    )(meta, *mixed_parts, tokens, cotangent, weights)
    block_out, middle_grad = middle[:2]
    do_made = middle[2 : 2 + NY]
    reduced_a = lax.psum_scatter(middle[3 + NY], "fsdp", scatter_dimension=0, tiled=True)
    reduced_a = lax.optimization_barrier(reduced_a)

    do_parts = [do_made[0]] + [shift_y(do_made[NY - k], k) for k in range(1, NY)]
    rest_cols = D + 128 + QCOLS
    back = pl.pallas_call(
        lambda *refs: back_kernel(nc, *refs),
        in_specs=[SMEM] + [VMEM] * (2 * NY + 7),
        out_specs=[VMEM] * (NY + nc),
        out_shape=[jax.ShapeDtypeStruct((ROWS, D), F32)]
        + [jax.ShapeDtypeStruct((ROWS, D), BF16)] * (NY - 1)
        + [jax.ShapeDtypeStruct((nz * nx, r24, rest_cols), BF16)] * nc,
        scratch_shapes=[
            pltpu.VMEM((HEADS, GROWS, HD), BF16),
            pltpu.VMEM((HEADS, GROWS, HD), F32),
            pltpu.VMEM((HEADS, GROWS, HD), F32),
            pltpu.VMEM((HEADS, GROWS, HD), F32),
            pltpu.VMEM((GROWS, WQ), BF16),
            pltpu.VMEM((GROWS, D), F32),
            pltpu.VMEM((128, D), F32),
            pltpu.VMEM((D, rest_cols), F32),
        ],
        compiler_params=params(60),
        cost_estimate=cost(12e9, 20e6),
        name="back",
    )(meta, *do_parts, *token_parts, qkv, lse, acts, wq, r0, kk, middle[2 + NY])
    dh_made = back[:NY]
    dh_parts = [dh_made[0]] + [shift_y(dh_made[NY - k], k) for k in range(1, NY)]

    def turns(parts, n, base, size):
        total = parts[0].shape
        return pl.pallas_call(
            lambda *refs: turns_kernel(n, base, *refs),
            in_specs=[SMEM] + [VMEM] * len(parts),
            out_specs=[VMEM] * n,
            out_shape=[jax.ShapeDtypeStruct((total[0] // n,) + total[1:], BF16)] * n,
            scratch_shapes=[pltpu.VMEM(total, F32)],
            compiler_params=params(24),
            name="turns",
        )(meta, *parts)

    parts = [back[NY]]
    if nc == 2:
        parts.append(shift_f(back[NY + 1], 0, 0, 1))
    made = turns(parts, nz, M_ZXY, nx)
    parts = [made[0]] + [shift_f(made[k], k, 0, 0) for k in range(1, nz)]
    parts, dh_parts = lax.optimization_barrier((parts, dh_parts))
    made = turns(parts, nx, M_ZXY + 1, 1)
    parts = [made[0]] + [shift_f(made[k], 0, k, 0) for k in range(1, nx)]
    made = pl.pallas_call(
        lambda *refs: rows_kernel(nx, r6, *refs),
        in_specs=[SMEM] + [VMEM] * nx,
        out_specs=[VMEM] * NY,
        out_shape=[jax.ShapeDtypeStruct((rows8, rest_cols + 128), BF16)] * NY,
        compiler_params=params(16),
        name="rows",
    )(meta, *[part[0] for part in parts])
    row_parts = [made[0]] + [shift_y(made[k], k) for k in range(1, NY)]
    c_heads = D + 128
    summed = sum(part.astype(F32) for part in row_parts)
    heads = jnp.stack([part[:r6, c_heads : c_heads + WQ] for part in row_parts])
    heads = jnp.concatenate([pick(heads, (y - q) % NY)[:, None] for q in range(NY)], axis=1)
    grad_qkv = heads.reshape(r6, NY, 3, HW).transpose(0, 2, 1, 3).reshape(r6, 3 * D).astype(F32)
    vecs = summed[:r6, D : D + 8]
    tail = summed[:r6, c_heads + WQ : c_heads + WQ + 4]
    grad_fcb = summed[:, rest_cols : rest_cols + groups].T.reshape(r24)
    tokens_grad = pl.pallas_call(
        end_kernel,
        in_specs=[VMEM] * (NY + 3),
        out_specs=VMEM,
        out_shape=jax.ShapeDtypeStruct((ROWS, D), BF16),
        compiler_params=params(24),
        cost_estimate=cost(1e7, 6e6),
        name="end",
    )(*dh_parts, tokens, middle_grad, gain_one)

    packed = jax.ShapeDtypeStruct((rows8, FF + groups * D), BF16)
    parts = pl.pallas_call(
        lambda *refs: split_kernel(r6, *refs),
        in_specs=[SMEM, VMEM],
        out_specs=[VMEM] * NY,
        out_shape=[packed] * NY,
        scratch_shapes=[pltpu.VMEM((NY, r24, D), F32)],
        compiler_params=params(60),
        name="split",
    )(meta, reduced_a)
    parts = [parts[0]] + [shift_y(parts[k], k) for k in range(1, NY)]
    grad_fc, grad_proj = pl.pallas_call(
        lambda *refs: join_kernel(count, r6, *refs),
        in_specs=[VMEM] * NY,
        out_specs=[VMEM] * 2,
        out_shape=[jax.ShapeDtypeStruct((r6, FF), F32), jax.ShapeDtypeStruct((r24, D), F32)],
        compiler_params=params(16),
        name="join",
    )(*parts)
    return (
        block_out,
        tokens_grad,
        tail[:, 0],
        tail[:, 1],
        grad_qkv,
        tail[:, 2:4].T.reshape(2 * r6),
        summed[:r6, :D],
        vecs[:, 4],
        vecs[:, 5],
        vecs[:, 6],
        grad_fc,
        grad_fcb,
        grad_proj,
        vecs[:, 7],
    )


def solution(mesh):
    both = P(("fsdp", "seq"))
    wide = P(("fsdp", "seq"), None)
    nz, nx, nc = (4, 4, 2) if mesh.shape["fsdp"] == 32 else (1, 1, mesh.shape["fsdp"])
    in_specs = (wide, P("fsdp"), P("fsdp"), P("fsdp", None), both, both, wide, both, wide)
    in_specs += (both, both, both, wide, both, wide, both, wide)
    out_specs = (wide, wide, both, both, wide, both, wide, both, both, both, wide, both, wide, both)

    def program(*args):
        return on_device(nz, nx, nc, *args)

    return jax.shard_map(
        program, mesh=mesh, in_specs=in_specs, out_specs=out_specs, check_vma=False
    )
```

```python
import numpy as np
import jax
import jax.numpy as jnp
from jax import lax
from jax.experimental import pallas as pl
from jax.experimental.pallas import tpu as pltpu
from jax.sharding import PartitionSpec as P

D = 768
H = 12
HD = 64
FF = 3072
BLK = 128
SLOTS = 3
NY = 4
GSLOTS = SLOTS * NY
ROWS = SLOTS * BLK
GROWS = GSLOTS * BLK
LONG = 8
LONG_LEN = LONG * BLK
HEADS = H // NY
HW = HEADS * HD
WQ = 3 * HW
QCOLS = 640
C_FC = 768
C_PROJ = C_FC + FF
C_VEC = C_PROJ + FF
WCOLS = C_VEC + 128
EPSILON = 1e-05
MASKED_SCORE = -1e30
SCALE = HD**-0.5
SEQ_STRIDE = 4096
M_INV, M_CODE, M_BASE, M_LIM, M_ZXY, M_THR, M_CORE = 0, 12, 16, 20, 24, 27, 30
F32 = jnp.float32
BF16 = jnp.bfloat16
TILES = tuple((256 * t, 0, 256 * (t + 1)) for t in range(4)) + ((1024, 1024, 256), (1280, 1024, 512))


def dot_nn(a, b):
    return lax.dot_general(a, b, (((1,), (0,)), ((), ())), preferred_element_type=F32)


def dot_nt(a, b):
    return lax.dot_general(a, b, (((1,), (1,)), ((), ())), preferred_element_type=F32)


def dot_tn(a, b):
    return lax.dot_general(a, b, (((0,), (0,)), ((), ())), preferred_element_type=F32)


def normed(value):
    center = jnp.mean(value, axis=-1, keepdims=True)
    offset = value - center
    spread = jnp.mean(offset * offset, axis=-1, keepdims=True)
    scale = lax.rsqrt(spread + EPSILON)
    return offset * scale, scale


def scaled(q):
    return (q.astype(F32) * SCALE).astype(BF16)


def minus(a, k, n):
    r = a - k
    return jnp.where(r < 0, r + n, r)


def visible_mask(meta, tile):
    q0, k0, count = tile
    row = lax.broadcasted_iota(jnp.int32, (256, 1), 0)
    col = lax.broadcasted_iota(jnp.int32, (1, count), 1)
    if q0 < LONG_LEN:
        return col <= row + q0
    first = (q0 - LONG_LEN) // BLK

    def per_slot(base, index, start, n):
        value = jnp.full(index.shape, meta[base + start], jnp.int32)
        for i in range(1, n):
            value = jnp.where(index >= i * BLK, meta[base + start + i], value)
        return value

    q_code = per_slot(M_CODE, row, first, 2) + (row & (BLK - 1))
    q_base = per_slot(M_BASE, row, first, 2)
    slots = count // BLK
    k_code = per_slot(M_CODE, col, 0, slots) + (col & (BLK - 1))
    k_lim = per_slot(M_LIM, col, 0, slots)
    k_code = jnp.where(k_code < k_lim, k_code, 1 << 24)
    return (k_code <= q_code) & (k_code >= q_base)


def select_matrix(r0, offset):
    rows = lax.broadcasted_iota(jnp.int32, (D, HW), 0)
    return jnp.where(rows == r0 + offset, 1.0, 0.0).astype(BF16)


def front_kernel(nz, nx, meta, *refs):
    x_refs, refs = refs[:NY], refs[NY:]
    z_refs, refs = refs[:nz], refs[nz:]
    r0_ref, k_ref = refs[:2]
    a1_hbm, qkv_hbm, lse_ref = refs[2:5]
    o_refs = refs[5 : 5 + NY]
    w_ref, gain_ref, oh, a1_ref, qkv_ref, sems = refs[5 + NY :]
    store_a1 = pltpu.make_async_copy(a1_ref, a1_hbm, sems.at[0])
    store_qkv = pltpu.make_async_copy(qkv_ref, qkv_hbm, sems.at[1])
    z, x, y = meta[M_ZXY], meta[M_ZXY + 1], meta[M_ZXY + 2]
    step = D // (nz * nx)
    for kz in range(nz):
        for kx in range(nx):
            at = (minus(z, kz, nz) * nx + minus(x, kx, nx)) * step
            w_ref[pl.ds(pl.multiple_of(at, step), step), :] = z_refs[kz][kx]
    vectors = jnp.transpose(w_ref[:, 512:640].astype(F32))
    gain = vectors[64:65]
    shift = vectors[65:66]
    gain_ref[...] = jnp.broadcast_to(gain, (8, D))
    small = vectors[64:72].astype(BF16)
    odd = k_ref[...] == 1
    sums = dot_nn(small, select_matrix(r0_ref[...], 96 * y))
    q_bias = jnp.where(odd, sums[3:4], sums[2:3])
    sums = dot_nn(small, select_matrix(r0_ref[...], 384 + 96 * y))
    v_bias = jnp.where(odd, sums[3:4], sums[2:3])
    bias = jnp.concatenate([q_bias, jnp.zeros((1, HW), F32), v_bias], axis=1)
    for k in range(NY):
        for j in range(SLOTS):
            hat, _ = normed(x_refs[k][j * BLK : (j + 1) * BLK, :].astype(F32))
            to = pl.multiple_of(meta[M_INV + k * SLOTS + j] * BLK, BLK)
            a1_ref[pl.ds(to, BLK), :] = (hat * gain + shift).astype(BF16)

    store_a1.start()

    def project(t, carry):
        rows = pl.ds(pl.multiple_of(t * 256, 256), 256)
        joined = (dot_nn(a1_ref[rows, :], w_ref[:, 0:WQ]) + bias).astype(BF16)
        for i in range(9):
            qkv_ref[i, rows, :] = joined[:, i * HD : (i + 1) * HD]
        return carry

    lax.fori_loop(0, GROWS // 256, project, 0)
    store_qkv.start()

    def head(h, carry):
        for tile in TILES:
            q0, k0, count = tile
            q = qkv_ref[h, q0 : q0 + 256, :]
            k = qkv_ref[HEADS + h, k0 : k0 + count, :]
            v = qkv_ref[2 * HEADS + h, k0 : k0 + count, :]
            scores = jnp.where(visible_mask(meta, tile), dot_nt(scaled(q), k), MASKED_SCORE)
            top = jnp.max(scores, axis=-1, keepdims=True)
            weights = jnp.exp(scores - top)
            total = jnp.sum(weights, axis=-1, keepdims=True)
            oh[h, q0 : q0 + 256, :] = dot_nn(weights.astype(BF16), v) * (1.0 / total)
            lse_ref[h, q0 : q0 + 256, :] = top + jnp.log(total)
        return carry

    lax.fori_loop(0, HEADS, head, 0)
    for k in range(NY):
        for j in range(SLOTS):
            rows = pl.ds(pl.multiple_of(meta[M_INV + k * SLOTS + j] * BLK, BLK), BLK)
            mixed = jnp.concatenate([oh[h, rows, :] for h in range(HEADS)], axis=1)
            o_refs[k][j * BLK : (j + 1) * BLK, :] = mixed.astype(BF16)
    store_a1.wait()
    store_qkv.wait()


GELU_C = float(np.sqrt(2.0 / np.pi))


def hidden_step(q, w, bias, a2, a2t, dz, acc, acc_da, g):
    at_fc = pl.ds(pl.multiple_of(q * D, D), D)
    at_p = pl.ds(pl.multiple_of((4 + q) * D, D), D)
    u = dot_nn(a2[...], w[:, at_fc]) + bias
    t = jnp.tanh(GELU_C * (u + 0.044715 * (u * u * u)))
    m = (0.5 * u * (1.0 + t)).astype(BF16)
    slope = 0.5 * (1.0 + t) + (0.5 * GELU_C) * u * (1.0 - t * t) * (1.0 + 0.134145 * (u * u))
    du = (dot_nt(dz[...], w[:, at_p]) * slope).astype(BF16)
    g[:, at_p] = dot_tn(m, dz[...]).astype(BF16)
    g[:, at_fc] = dot_nn(a2t[...], du).astype(BF16)
    acc[...] += dot_nn(m, w[:, at_p])
    acc_da[...] += dot_nt(du, w[:, at_fc])
    return jnp.sum(du.astype(F32), axis=0, keepdims=True)


def middle_kernel(meta, *refs):
    o_refs, refs = refs[:NY], refs[NY:]
    x_ref, cot_ref, w_hbm = refs[:3]
    out_ref, dy_ref = refs[3:5]
    do_refs, refs = refs[5 : 5 + NY], refs[5 + NY :]
    rest, g_hbm, w, g, gw, hat2, dz, a2, a2t, acc, acc_da, gvec, vec_s, sems = refs
    y = meta[M_ZXY + 2]

    def load(i, at, to, n):
        return pltpu.make_async_copy(w_hbm.at[:, pl.ds(at, n)], w.at[:, pl.ds(to, n)], sems.at[i])

    def load_fc(q):
        return load(2 + q, pl.multiple_of(C_FC + q * D, D), pl.multiple_of(q * D, D), D)

    def load_proj(q):
        return load(6 + q, pl.multiple_of(C_PROJ + q * D, D), pl.multiple_of((4 + q) * D, D), D)

    def store(i):
        at = pl.ds(pl.multiple_of(i * D, D), D)
        return pltpu.make_async_copy(g.at[:, at], g_hbm.at[:, at], sems.at[10 + i])

    firsts = [load(0, 0, 8 * D, D), load(1, C_VEC, 9 * D, 128)]
    for copy in firsts:
        copy.start()
    for q in range(4):
        load_fc(q).start()
        load_proj(q).start()
    offset = lax.broadcasted_iota(jnp.int32, (BLK, 1), 0)
    for j in range(SLOTS):
        rows = slice(j * BLK, (j + 1) * BLK)
        live = jnp.where(offset < meta[M_THR + j], 1.0, 0.0)
        dz[rows, :] = (cot_ref[rows, :].astype(F32) * live).astype(BF16)
    for copy in firsts:
        copy.wait()
    vec = jnp.transpose(w[:, 9 * D : 9 * D + 128].astype(F32))
    vec_s[...] = vec
    total = x_ref[...].astype(F32) + vec[4:5, :]
    for k in range(NY):
        at = pl.ds(pl.multiple_of(minus(y, k, NY) * HW, HW), HW)
        total = total + dot_nn(o_refs[k][...], w[at, 8 * D : 9 * D])
    hat, scale = normed(total)
    hat2[...] = hat
    acts = hat * vec[5:6, :] + vec[6:7, :]
    a2[...] = acts.astype(BF16)
    a2t[...] = jnp.transpose(acts).astype(BF16)
    acc[...] = total + vec[7:8, :]
    acc_da[...] = jnp.zeros_like(acc_da)
    gvec[...] = jnp.zeros_like(gvec)

    def step(q, carry):
        load_fc(q).wait()
        load_proj(q).wait()
        at = pl.ds(8 + q, 1)
        gvec[at, :] = hidden_step(q, w, vec_s[at, :], a2, a2t, dz, acc, acc_da, g)
        store(q).start()
        store(4 + q).start()
        return carry

    lax.fori_loop(0, 4, step, 0)
    out_ref[...] = acc[...].astype(BF16)
    da2 = acc_da[...]
    hat = hat2[...]
    gvec[6:7, :] = jnp.sum(da2, axis=0, keepdims=True)
    gvec[5:6, :] = jnp.sum(da2 * hat, axis=0, keepdims=True)
    dhat = da2 * vec[5:6, :]
    mean_a = jnp.mean(dhat, axis=-1, keepdims=True)
    mean_b = jnp.mean(dhat * hat, axis=-1, keepdims=True)
    dz32 = dz[...].astype(F32)
    dy = dz32 + scale * (dhat - mean_a - hat * mean_b)
    dy_ref[...] = dy
    da = dy.astype(BF16)
    gvec[7:8, :] = jnp.sum(dz32, axis=0, keepdims=True)
    gvec[4:5, :] = jnp.sum(da.astype(F32), axis=0, keepdims=True)
    for k in range(NY):
        at = pl.ds(pl.multiple_of(minus(y, k, NY) * HW, HW), HW)
        do_refs[k][...] = dot_nt(da, w[at, 8 * D : 9 * D]).astype(BF16)
        gw[at, :] = dot_tn(o_refs[k][...], da)
    rest[:, 0:D] = gw[...].astype(BF16)
    rest[:, D : D + 128] = jnp.transpose(gvec[...]).astype(BF16)
    for i in range(8):
        store(i).wait()


def hidden_order(count, r24):
    return [
        (d * 4 * r24 + q * r24, (q * count + d) * r24) for q in range(NY) for d in range(count)
    ]


def pack_kernel(count, r6, *refs):
    sources, out, wide, vec = refs[:12], refs[12], refs[13], refs[14]
    local, sems = refs[15:27], refs[27]
    loads = [
        pltpu.make_async_copy(source, local[i], sems.at[i]) for i, source in enumerate(sources)
    ]
    for load in loads:
        load.start()
    r24 = NY * r6
    rows = out.shape[0]
    out[...] = jnp.zeros_like(out)
    vec[...] = jnp.zeros_like(vec)
    for load in loads:
        load.wait()
    wq, wo, wf, wp, g1, b1, qv, ob, g2, b2, fb, pb = local
    out[0:r6, 0 : 3 * D] = wq[...]
    out[0:r6, 3 * D : 4 * D] = wo[...]
    value = wf[...].astype(F32)
    for natural, packed in hidden_order(count, r24):
        wide[:, packed : packed + r24] = value[:, natural : natural + r24]
    out[0:r6, 4 * D : 4 * D + FF] = wide[...].astype(BF16)
    value = wp[...].astype(F32)
    for i in range(r24 // rows):
        at = 4 * D + FF + i * D
        out[:, at : at + D] = value[i * rows : (i + 1) * rows, :].astype(BF16)
    vec[0:1, 0:r6] = g1[...].astype(F32)
    vec[1:2, 0:r6] = b1[...].astype(F32)
    both = qv[...].astype(F32)
    vec[2:3, 0:r6] = both[:, 0:r6]
    vec[3:4, 0:r6] = both[:, r6 : 2 * r6]
    vec[4:5, 0:r6] = ob[...].astype(F32)
    vec[5:6, 0:r6] = g2[...].astype(F32)
    vec[6:7, 0:r6] = b2[...].astype(F32)
    vec[7:8, 0:r6] = pb[...].astype(F32)
    hidden = fb[...].astype(F32)
    for i in range(r24 // rows):
        vec[8 + i : 9 + i, 0:rows] = hidden[:, i * rows : (i + 1) * rows]
    at = out.shape[1] - 128
    out[:, at : at + 128] = jnp.transpose(vec[...])[0:rows, :].astype(BF16)


def turns_kernel(n, base, meta, *refs):
    parts, outs, total = refs[: -n - 1], refs[-n - 1 : -1], refs[-1]
    value = parts[0][...].astype(F32)
    for part in parts[1:]:
        value = value + part[...].astype(F32)
    total[...] = value
    size = total.shape[0] // n
    for k in range(n):
        at = lax.rem(meta[base] + k, n) * size
        outs[k][...] = total[pl.ds(at, size)].astype(BF16)


def rows_kernel(n, r6, meta, *refs):
    parts, outs = refs[:n], refs[n:]
    total = parts[0][...].astype(F32)
    for part in parts[1:]:
        total = total + part[...].astype(F32)
    y = meta[M_ZXY + 2]
    r24, width = total.shape
    rows = outs[0].shape[0]
    i = lax.broadcasted_iota(jnp.int32, (rows, r24), 0)
    j = lax.broadcasted_iota(jnp.int32, (rows, r24), 1)
    lane = lax.broadcasted_iota(jnp.int32, (rows, 128), 1)
    value = total.astype(BF16)
    bias = value[:, D : D + 128]
    for k in range(NY):
        to = lax.rem(y + k, NY)
        chosen = jnp.where((i < r6) & (j == i + to * r6), 1.0, 0.0).astype(BF16)
        outs[k][:, 0:width] = dot_nn(chosen, value).astype(BF16)
        hidden = jnp.zeros((rows, 128), F32)
        for g in range(r24 // rows):
            group = dot_nn(jnp.where(j == i + g * rows, 1.0, 0.0).astype(BF16), bias)
            column = jnp.sum(jnp.where(lane == 8 + to, group, 0.0), axis=1, keepdims=True)
            hidden = hidden + jnp.where(lane == g, column, 0.0)
        outs[k][:, width : width + 128] = hidden.astype(BF16)


def split_kernel(r6, meta, reduced, *refs):
    outs, (blocks,) = refs[:NY], refs[NY:]
    r24 = NY * r6
    rows = outs[0].shape[0]
    y = meta[M_ZXY + 2]
    for q in range(NY):
        blocks[q] = reduced[:, FF + q * D : FF + (q + 1) * D].astype(F32)
    i = lax.broadcasted_iota(jnp.int32, (rows, r24), 0)
    j = lax.broadcasted_iota(jnp.int32, (rows, r24), 1)
    for k in range(NY):
        to = lax.rem(y + k, NY)
        chosen = jnp.where((i < r6) & (j == i + to * r6), 1.0, 0.0).astype(BF16)
        outs[k][:, 0:FF] = dot_nn(chosen, reduced[:, 0:FF]).astype(BF16)
        value = blocks[to]
        for n in range(r24 // rows):
            outs[k][:, FF + n * D : FF + (n + 1) * D] = value[n * rows : (n + 1) * rows, :].astype(
                BF16
            )


def join_kernel(count, r6, *refs):
    parts, (fc, proj) = refs[:NY], refs[NY:]
    r24 = NY * r6
    rows = parts[0].shape[0]
    total = parts[0][...].astype(F32)
    for k in range(1, NY):
        total = total + parts[k][...].astype(F32)
    for natural, packed in hidden_order(count, r24):
        fc[:, natural : natural + r24] = total[0:r6, packed : packed + r24]
    for n in range(r24 // rows):
        proj[n * rows : (n + 1) * rows, :] = total[:, FF + n * D : FF + (n + 1) * D]


def back_kernel(nc, meta, *refs):
    do_refs, refs = refs[:NY], refs[NY:]
    x_hbm, refs = refs[:NY], refs[NY:]
    qkv_ref, lse_ref, a1_hbm, w_hbm, r0_ref, k_ref, rest_hbm = refs[:7]
    dh_refs, refs = refs[7 : 7 + NY], refs[7 + NY :]
    halves, refs = refs[:nc], refs[nc:]
    doh, dq, dk, dv, dqkv, dh, gvec, gq_ref, w_ref, x_refs, a1_ref, rest, sems = refs
    pairs = [(w_hbm, w_ref), (a1_hbm, a1_ref), (rest_hbm, rest)]
    pairs += [(x_hbm[k], x_refs.at[k]) for k in range(NY)]
    loads = [pltpu.make_async_copy(a, b, sems.at[i]) for i, (a, b) in enumerate(pairs)]
    for load in loads:
        load.start()
    y = meta[M_ZXY + 2]
    for k in range(NY):
        for j in range(SLOTS):
            rows = pl.ds(pl.multiple_of(meta[M_INV + k * SLOTS + j] * BLK, BLK), BLK)
            piece = do_refs[k][j * BLK : (j + 1) * BLK, :]
            for h in range(HEADS):
                doh[h, rows, :] = piece[:, h * HD : (h + 1) * HD]
    dk[...] = jnp.zeros_like(dk)
    dv[...] = jnp.zeros_like(dv)

    def head(h, carry):
        for tile in TILES:
            q0, k0, count = tile
            q = qkv_ref[h, q0 : q0 + 256, :]
            k = qkv_ref[HEADS + h, k0 : k0 + count, :]
            v = qkv_ref[2 * HEADS + h, k0 : k0 + count, :]
            do = doh[h, q0 : q0 + 256, :]
            q = scaled(q)
            scores = jnp.where(visible_mask(meta, tile), dot_nt(q, k), MASKED_SCORE)
            probs = jnp.exp(scores - lse_ref[h, q0 : q0 + 256, :])
            dp = dot_nt(do, v)
            row_dot = jnp.sum(dp * probs, axis=-1, keepdims=True)
            ds = (probs * (dp - row_dot)).astype(BF16)
            dq[h, q0 : q0 + 256, :] = dot_nn(ds, k) * SCALE
            dk[h, k0 : k0 + count, :] += dot_tn(ds, q)
            dv[h, k0 : k0 + count, :] += dot_tn(probs.astype(BF16), do)
        return carry

    lax.fori_loop(0, HEADS, head, 0)

    for load in loads:
        load.wait()

    def join(t, carry):
        rows = pl.ds(pl.multiple_of(t * 256, 256), 256)
        parts = [dq[h, rows, :] for h in range(HEADS)]
        parts += [dk[h, rows, :] for h in range(HEADS)]
        parts += [dv[h, rows, :] for h in range(HEADS)]
        joined = jnp.concatenate(parts, axis=1).astype(BF16)
        dqkv[rows, :] = joined
        dh[rows, :] = dot_nt(joined, w_ref[:, 0:WQ])
        return carry + jnp.sum(joined.astype(F32), axis=0, keepdims=True)

    sums = lax.fori_loop(0, GROWS // 256, join, jnp.zeros((1, WQ), F32))
    gain_sum = jnp.zeros((1, D), F32)
    shift_sum = jnp.zeros((1, D), F32)
    for k in range(NY):
        for j in range(SLOTS):
            rows = pl.ds(pl.multiple_of(meta[M_INV + k * SLOTS + j] * BLK, BLK), BLK)
            here = slice(j * BLK, (j + 1) * BLK)
            value = dh[rows, :]
            hat, _ = normed(x_refs[k, here, :].astype(F32))
            gain_sum += jnp.sum(value * hat, axis=0, keepdims=True)
            shift_sum += jnp.sum(value, axis=0, keepdims=True)
            dh_refs[k][here, :] = value.astype(dh_refs[k].dtype)
    gvec[...] = jnp.zeros_like(gvec)
    gvec[64:65, :] = gain_sum
    gvec[65:66, :] = shift_sum
    q_sum = sums[:, 0:HW]
    v_sum = sums[:, 2 * HW : 3 * HW]
    odd = k_ref[...] == 1
    for i in range(2):
        keep = odd if i else jnp.logical_not(odd)
        row = jnp.zeros((8, D), F32)
        for part, start in ((q_sum, 0), (v_sum, 384)):
            value = jnp.broadcast_to(jnp.where(keep, part, 0.0), (8, HW)).astype(BF16)
            row = row + dot_nt(value, select_matrix(r0_ref[...], start + 96 * y))
        gvec[66 + i : 67 + i, :] = row[0:1]

    def grads(c, carry):
        rows = pl.ds(pl.multiple_of(c * 256, 256), 256)
        gq_ref[rows, D + 128 : D + 128 + WQ] = dot_tn(a1_ref[:, rows], dqkv[...])
        return carry

    lax.fori_loop(0, 3, grads, 0)
    gq_ref[:, 0 : D + 128] = rest[...].astype(F32)
    gq_ref[:, D + 128 + WQ :] = jnp.transpose(gvec[...])[:, 64:128]
    blocks, size = halves[0].shape[:2]
    for k in range(nc):
        core = lax.rem(meta[M_CORE] + k, nc) * size
        for i in range(blocks):
            at = pl.multiple_of(i * size * nc + core, 8)
            halves[k][i] = gq_ref[pl.ds(at, size), :].astype(BF16)


def end_kernel(*refs):
    dh_refs = refs[:NY]
    x_ref, dy_ref, gain_ref, out_ref = refs[NY:]
    dh = dh_refs[0][...]
    for k in range(1, NY):
        dh = dh + dh_refs[k][...].astype(F32)
    hat, scale = normed(x_ref[...].astype(F32))
    dhat = dh * gain_ref[0:1, :]
    mean_a = jnp.mean(dhat, axis=-1, keepdims=True)
    mean_b = jnp.mean(dhat * hat, axis=-1, keepdims=True)
    out_ref[...] = (dy_ref[...] + scale * (dhat - mean_a - hat * mean_b)).astype(BF16)


def params(mib):
    return pltpu.CompilerParams(vmem_limit_bytes=mib * 2**20)


VMEM = pl.BlockSpec(memory_space=pltpu.VMEM)
SMEM = pl.BlockSpec(memory_space=pltpu.SMEM)
HBM = pl.BlockSpec(memory_space=pltpu.HBM)


def cost(flops, nbytes):
    return pl.CostEstimate(flops=int(flops), bytes_accessed=int(nbytes), transcendentals=0)


def on_device(
    nz,
    nx,
    nc,
    tokens,
    slot_seq,
    slot_block_index,
    lengths,
    ln1_gain,
    ln1_bias,
    w_qkv,
    qv_bias,
    w_out,
    out_bias,
    ln2_gain,
    ln2_bias,
    w_fc,
    feed_input_bias,
    w_proj,
    proj_bias,
    cotangent,
):
    r6 = w_qkv.shape[0]
    r24 = NY * r6
    count = nz * nx * nc
    y = lax.axis_index("seq")
    f = lax.axis_index("fsdp")
    z, x, c = f // (nx * nc), (f // nc) % nx, f % nc

    def shift_y(value, k):
        return lax.ppermute(value, "seq", [(i, (i + k) % NY) for i in range(NY)])

    def shift_f(value, dz, dx, dc):
        pairs = []
        for i in range(count):
            iz, ix, ic = i // (nx * nc), (i // nc) % nx, i % nc
            to = (((iz + dz) % nz) * nx + (ix + dx) % nx) * nc + (ic + dc) % nc
            pairs.append((i, to))
        return lax.ppermute(value, "fsdp", pairs)

    def pick(value, i, axis=0):
        return lax.dynamic_index_in_dim(value, i, axis, keepdims=False)

    rel = np.arange(GSLOTS)
    absolute = ((y - rel // SLOTS) % NY) * SLOTS + rel % SLOTS
    chosen = absolute[:, None] == np.arange(GSLOTS)[None, :]
    seqs = jnp.sum(jnp.where(chosen, slot_seq[None, :], 0), axis=1)
    blocks = jnp.sum(jnp.where(chosen, slot_block_index[None, :], 0), axis=1)
    lens = jnp.sum(
        jnp.where(seqs[:, None] == np.arange(lengths.shape[1])[None, :], lengths[0:1, :], 0), axis=1
    )
    order = jnp.where(lens == LONG_LEN, 0, (seqs + 1) * 16) + blocks
    inverse = jnp.sum((order[None, :] < order[:, None]).astype(jnp.int32), axis=1)
    short = inverse[None, :] == (LONG + np.arange(4))[:, None]
    codes = jnp.sum(jnp.where(short, (seqs * SEQ_STRIDE + blocks * BLK)[None, :], 0), axis=1)
    bases = jnp.sum(jnp.where(short, (seqs * SEQ_STRIDE)[None, :], 0), axis=1)
    limits = jnp.sum(jnp.where(short, (seqs * SEQ_STRIDE + lens)[None, :], 0), axis=1)
    place = jnp.stack([z, x, y]).astype(jnp.int32)
    alive = (lens - blocks * BLK)[:SLOTS]
    core = jnp.stack([c, jnp.zeros_like(c)]).astype(jnp.int32)
    meta = jnp.concatenate([inverse, codes, bases, limits, place, alive, core])
    lane = np.arange(HW)
    r0 = jnp.asarray(((lane // (2 * r6)) * r6 + lane % r6)[None, :], jnp.int32)
    kk = jnp.asarray(((lane // r6) % 2)[None, :], jnp.int32)

    rows8 = (r6 + 7) // 8 * 8
    groups = r24 // rows8
    width = 4 * D + FF + groups * D + 128
    vectors = (ln1_gain, ln1_bias, qv_bias, out_bias, ln2_gain, ln2_bias, feed_input_bias, proj_bias)
    sources = [w_qkv, w_out, w_fc, w_proj] + [v[None, :] for v in vectors]
    payload = pl.pallas_call(
        lambda *refs: pack_kernel(count, r6, *refs),
        in_specs=[HBM] * 12,
        out_specs=VMEM,
        out_shape=jax.ShapeDtypeStruct((rows8, width), BF16),
        scratch_shapes=[pltpu.VMEM((r6, FF), F32), pltpu.VMEM((128, max(128, rows8)), F32)]
        + [pltpu.VMEM(v.shape, BF16) for v in sources]
        + [pltpu.SemaphoreType.DMA((12,))],
        compiler_params=params(60),
        name="pack",
    )(*sources)
    payloads = [payload] + [shift_y(payload, k) for k in range(1, NY)]
    later, _ = lax.optimization_barrier((tokens, payload))
    token_parts = [tokens] + [shift_y(later, k) for k in range(1, NY)]
    spread = jnp.stack(payloads)
    spread = jnp.concatenate([pick(spread, (y - q) % NY)[None] for q in range(NY)])
    v0 = width - 128
    vec_rows = spread[:, :r6, v0 : v0 + 8].reshape(r24, 8)
    qkv_mine = pick(spread[:, :r6, : 3 * D].reshape(r24, 3, NY, HW), y, 2).reshape(r24, WQ)
    wq_local = jnp.concatenate([qkv_mine, vec_rows, jnp.zeros((r24, 56), BF16)], axis=1)
    proj_rows = jnp.concatenate(
        [
            jnp.concatenate(
                [
                    spread[q, :, 4 * D + FF + n * D : 4 * D + FF + (n + 1) * D]
                    for n in range(groups)
                ],
                axis=0,
            )
            for q in range(NY)
        ],
        axis=1,
    )
    fcb_rows = jnp.transpose(spread[:, :, v0 + 8 : v0 + 8 + groups], (2, 1, 0)).reshape(r24, NY)
    w_local = jnp.concatenate(
        [
            spread[:, :r6, 3 * D : 4 * D + FF].reshape(r24, D + FF),
            proj_rows,
            vec_rows,
            fcb_rows,
            jnp.zeros((r24, 116), BF16),
        ],
        axis=1,
    )
    weights = lax.all_gather(w_local, "fsdp", axis=0, tiled=True)

    pair = wq_local
    if nc == 2:
        other = shift_f(wq_local, 0, 0, 1)
        first = jnp.where(c == 0, wq_local, other)
        second = jnp.where(c == 0, other, wq_local)
        pair = jnp.concatenate([first, second], axis=0)
    line = jnp.stack([pair] + [shift_f(pair, 0, k, 0) for k in range(1, nx)])
    planes = [line] + [shift_f(line, k, 0, 0) for k in range(1, nz)]

    front = pl.pallas_call(
        lambda *refs: front_kernel(nz, nx, *refs),
        in_specs=[SMEM] + [VMEM] * (NY + nz + 2),
        out_specs=[HBM] * 2 + [VMEM] * (3 + NY),
        out_shape=[
            jax.ShapeDtypeStruct((GROWS, D), BF16),
            jax.ShapeDtypeStruct((9, GROWS, HD), BF16),
            jax.ShapeDtypeStruct((HEADS, GROWS, 1), F32),
        ]
        + [jax.ShapeDtypeStruct((ROWS, HW), BF16)] * NY
        + [jax.ShapeDtypeStruct((D, QCOLS), BF16), jax.ShapeDtypeStruct((8, D), F32)],
        scratch_shapes=[
            pltpu.VMEM((HEADS, GROWS, HD), F32),
            pltpu.VMEM((GROWS, D), BF16),
            pltpu.VMEM((9, GROWS, HD), BF16),
            pltpu.SemaphoreType.DMA((2,)),
        ],
        compiler_params=params(60),
        cost_estimate=cost(8e9, 15e6),
        name="front",
    )(meta, *token_parts, *planes, r0, kk)
    acts, qkv, lse = front[:3]
    mixed = front[3 : 3 + NY]
    wq, gain_one = front[3 + NY :]

    mixed_parts = [mixed[0]] + [shift_y(mixed[NY - k], k) for k in range(1, NY)]
    wide32 = jax.ShapeDtypeStruct((ROWS, D), F32)
    wide16 = jax.ShapeDtypeStruct((ROWS, D), BF16)
    middle = pl.pallas_call(
        middle_kernel,
        in_specs=[SMEM] + [VMEM] * (NY + 2) + [HBM],
        out_specs=[VMEM] * (3 + NY) + [HBM],
        out_shape=[wide16, wide32]
        + [jax.ShapeDtypeStruct((ROWS, HW), BF16)] * NY
        + [
            jax.ShapeDtypeStruct((D, D + 128), BF16),
            jax.ShapeDtypeStruct((D, 8 * D), BF16),
        ],
        scratch_shapes=[
            pltpu.VMEM((D, 9 * D + 128), BF16),
            pltpu.VMEM((D, 8 * D), BF16),
            pltpu.VMEM((D, D), F32),
            pltpu.VMEM((ROWS, D), F32),
            pltpu.VMEM((ROWS, D), BF16),
            pltpu.VMEM((ROWS, D), BF16),
            pltpu.VMEM((D, ROWS), BF16),
            pltpu.VMEM((ROWS, D), F32),
            pltpu.VMEM((ROWS, D), F32),
            pltpu.VMEM((128, D), F32),
            pltpu.VMEM((128, D), F32),
            pltpu.SemaphoreType.DMA((18,)),
        ],
        compiler_params=params(60),
        cost_estimate=cost(13e9, 28e6),
        name="middle",
    )(meta, *mixed_parts, tokens, cotangent, weights)
    block_out, middle_grad = middle[:2]
    do_made = middle[2 : 2 + NY]
    reduced_a = lax.psum_scatter(middle[3 + NY], "fsdp", scatter_dimension=0, tiled=True)
    reduced_a = lax.optimization_barrier(reduced_a)

    do_parts = [do_made[0]] + [shift_y(do_made[NY - k], k) for k in range(1, NY)]
    rest_cols = D + 128 + QCOLS
    back = pl.pallas_call(
        lambda *refs: back_kernel(nc, *refs),
        in_specs=[SMEM] + [VMEM] * NY + [HBM] * NY + [VMEM] * 2 + [HBM] * 2 + [VMEM] * 2 + [HBM],
        out_specs=[VMEM] * (NY + nc),
        out_shape=[jax.ShapeDtypeStruct((ROWS, D), F32)]
        + [jax.ShapeDtypeStruct((ROWS, D), BF16)] * (NY - 1)
        + [jax.ShapeDtypeStruct((nz * nx, r24, rest_cols), BF16)] * nc,
        scratch_shapes=[
            pltpu.VMEM((HEADS, GROWS, HD), BF16),
            pltpu.VMEM((HEADS, GROWS, HD), F32),
            pltpu.VMEM((HEADS, GROWS, HD), F32),
            pltpu.VMEM((HEADS, GROWS, HD), F32),
            pltpu.VMEM((GROWS, WQ), BF16),
            pltpu.VMEM((GROWS, D), F32),
            pltpu.VMEM((128, D), F32),
            pltpu.VMEM((D, rest_cols), F32),
            pltpu.VMEM((D, QCOLS), BF16),
            pltpu.VMEM((NY, ROWS, D), BF16),
            pltpu.VMEM((GROWS, D), BF16),
            pltpu.VMEM((D, D + 128), BF16),
            pltpu.SemaphoreType.DMA((7,)),
        ],
        compiler_params=params(60),
        cost_estimate=cost(12e9, 20e6),
        name="back",
    )(meta, *do_parts, *token_parts, qkv, lse, acts, wq, r0, kk, middle[2 + NY])
    dh_made = back[:NY]
    dh_parts = [dh_made[0]] + [shift_y(dh_made[NY - k], k) for k in range(1, NY)]

    def turns(parts, n, base, size):
        total = parts[0].shape
        return pl.pallas_call(
            lambda *refs: turns_kernel(n, base, *refs),
            in_specs=[SMEM] + [VMEM] * len(parts),
            out_specs=[VMEM] * n,
            out_shape=[jax.ShapeDtypeStruct((total[0] // n,) + total[1:], BF16)] * n,
            scratch_shapes=[pltpu.VMEM(total, F32)],
            compiler_params=params(24),
            name="turns",
        )(meta, *parts)

    parts = [back[NY]]
    if nc == 2:
        parts.append(shift_f(back[NY + 1], 0, 0, 1))
    made = turns(parts, nz, M_ZXY, nx)
    parts = [made[0]] + [shift_f(made[k], k, 0, 0) for k in range(1, nz)]
    parts, dh_parts = lax.optimization_barrier((parts, dh_parts))
    made = turns(parts, nx, M_ZXY + 1, 1)
    parts = [made[0]] + [shift_f(made[k], 0, k, 0) for k in range(1, nx)]
    made = pl.pallas_call(
        lambda *refs: rows_kernel(nx, r6, *refs),
        in_specs=[SMEM] + [VMEM] * nx,
        out_specs=[VMEM] * NY,
        out_shape=[jax.ShapeDtypeStruct((rows8, rest_cols + 128), BF16)] * NY,
        compiler_params=params(16),
        name="rows",
    )(meta, *[part[0] for part in parts])
    row_parts = [made[0]] + [shift_y(made[k], k) for k in range(1, NY)]
    c_heads = D + 128
    summed = sum(part.astype(F32) for part in row_parts)
    heads = jnp.stack([part[:r6, c_heads : c_heads + WQ] for part in row_parts])
    heads = jnp.concatenate([pick(heads, (y - q) % NY)[:, None] for q in range(NY)], axis=1)
    grad_qkv = heads.reshape(r6, NY, 3, HW).transpose(0, 2, 1, 3).reshape(r6, 3 * D).astype(F32)
    vecs = summed[:r6, D : D + 8]
    tail = summed[:r6, c_heads + WQ : c_heads + WQ + 4]
    grad_fcb = summed[:, rest_cols : rest_cols + groups].T.reshape(r24)
    tokens_grad = pl.pallas_call(
        end_kernel,
        in_specs=[VMEM] * (NY + 3),
        out_specs=VMEM,
        out_shape=jax.ShapeDtypeStruct((ROWS, D), BF16),
        compiler_params=params(24),
        cost_estimate=cost(1e7, 6e6),
        name="end",
    )(*dh_parts, tokens, middle_grad, gain_one)

    packed = jax.ShapeDtypeStruct((rows8, FF + groups * D), BF16)
    parts = pl.pallas_call(
        lambda *refs: split_kernel(r6, *refs),
        in_specs=[SMEM, VMEM],
        out_specs=[VMEM] * NY,
        out_shape=[packed] * NY,
        scratch_shapes=[pltpu.VMEM((NY, r24, D), F32)],
        compiler_params=params(60),
        name="split",
    )(meta, reduced_a)
    parts = [parts[0]] + [shift_y(parts[k], k) for k in range(1, NY)]
    grad_fc, grad_proj = pl.pallas_call(
        lambda *refs: join_kernel(count, r6, *refs),
        in_specs=[VMEM] * NY,
        out_specs=[VMEM] * 2,
        out_shape=[jax.ShapeDtypeStruct((r6, FF), F32), jax.ShapeDtypeStruct((r24, D), F32)],
        compiler_params=params(16),
        name="join",
    )(*parts)
    return (
        block_out,
        tokens_grad,
        tail[:, 0],
        tail[:, 1],
        grad_qkv,
        tail[:, 2:4].T.reshape(2 * r6),
        summed[:r6, :D],
        vecs[:, 4],
        vecs[:, 5],
        vecs[:, 6],
        grad_fc,
        grad_fcb,
        grad_proj,
        vecs[:, 7],
    )


def solution(mesh):
    both = P(("fsdp", "seq"))
    wide = P(("fsdp", "seq"), None)
    nz, nx, nc = (4, 4, 2) if mesh.shape["fsdp"] == 32 else (1, 1, mesh.shape["fsdp"])
    in_specs = (wide, P("fsdp"), P("fsdp"), P("fsdp", None), both, both, wide, both, wide)
    in_specs += (both, both, both, wide, both, wide, both, wide)
    out_specs = (wide, wide, both, both, wide, both, wide, both, both, both, wide, both, wide, both)

    def program(*args):
        return on_device(nz, nx, nc, *args)

    return jax.shard_map(
        program, mesh=mesh, in_specs=in_specs, out_specs=out_specs, check_vma=False
    )
```

```python
import numpy as np
import jax
import jax.numpy as jnp
from jax import lax
from jax.experimental import pallas as pl
from jax.experimental.pallas import tpu as pltpu
from jax.sharding import PartitionSpec as P

D = 768
H = 12
HD = 64
FF = 3072
BLK = 128
SLOTS = 3
NY = 4
GSLOTS = SLOTS * NY
ROWS = SLOTS * BLK
GROWS = GSLOTS * BLK
LONG = 8
LONG_LEN = LONG * BLK
HEADS = H // NY
HW = HEADS * HD
WQ = 3 * HW
QCOLS = 640
C_FC = 768
C_PROJ = C_FC + FF
C_VEC = C_PROJ + FF
WCOLS = C_VEC + 128
EPSILON = 1e-05
MASKED_SCORE = -1e30
SCALE = HD**-0.5
SEQ_STRIDE = 4096
M_INV, M_CODE, M_BASE, M_LIM, M_ZXY, M_THR, M_CORE = 0, 12, 16, 20, 24, 27, 30
F32 = jnp.float32
BF16 = jnp.bfloat16
TILES = tuple((256 * t, 0, 256 * (t + 1)) for t in range(4)) + ((1024, 1024, 256), (1280, 1024, 512))


def dot_nn(a, b):
    return lax.dot_general(a, b, (((1,), (0,)), ((), ())), preferred_element_type=F32)


def dot_nt(a, b):
    return lax.dot_general(a, b, (((1,), (1,)), ((), ())), preferred_element_type=F32)


def dot_tn(a, b):
    return lax.dot_general(a, b, (((0,), (0,)), ((), ())), preferred_element_type=F32)


def normed(value):
    center = jnp.mean(value, axis=-1, keepdims=True)
    offset = value - center
    spread = jnp.mean(offset * offset, axis=-1, keepdims=True)
    scale = lax.rsqrt(spread + EPSILON)
    return offset * scale, scale


def scaled(q):
    return (q.astype(F32) * SCALE).astype(BF16)


def minus(a, k, n):
    r = a - k
    return jnp.where(r < 0, r + n, r)


def visible_mask(meta, tile):
    q0, k0, count = tile
    row = lax.broadcasted_iota(jnp.int32, (256, 1), 0)
    col = lax.broadcasted_iota(jnp.int32, (1, count), 1)
    if q0 < LONG_LEN:
        return col <= row + q0
    first = (q0 - LONG_LEN) // BLK

    def per_slot(base, index, start, n):
        value = jnp.full(index.shape, meta[base + start], jnp.int32)
        for i in range(1, n):
            value = jnp.where(index >= i * BLK, meta[base + start + i], value)
        return value

    q_code = per_slot(M_CODE, row, first, 2) + (row & (BLK - 1))
    q_base = per_slot(M_BASE, row, first, 2)
    slots = count // BLK
    k_code = per_slot(M_CODE, col, 0, slots) + (col & (BLK - 1))
    k_lim = per_slot(M_LIM, col, 0, slots)
    k_code = jnp.where(k_code < k_lim, k_code, 1 << 24)
    return (k_code <= q_code) & (k_code >= q_base)


def select_matrix(r0, offset):
    rows = lax.broadcasted_iota(jnp.int32, (D, HW), 0)
    return jnp.where(rows == r0 + offset, 1.0, 0.0).astype(BF16)


def front_kernel(nz, nx, meta, *refs):
    x_refs, refs = refs[:NY], refs[NY:]
    z_refs, refs = refs[:nz], refs[nz:]
    r0_ref, k_ref = refs[:2]
    a1_hbm, qkv_hbm, lse_ref = refs[2:5]
    o_refs = refs[5 : 5 + NY]
    w_ref, gain_ref, oh, a1_ref, qkv_ref, sems = refs[5 + NY :]
    store_a1 = pltpu.make_async_copy(a1_ref, a1_hbm, sems.at[0])
    store_qkv = pltpu.make_async_copy(qkv_ref, qkv_hbm, sems.at[1])
    z, x, y = meta[M_ZXY], meta[M_ZXY + 1], meta[M_ZXY + 2]
    step = D // (nz * nx)
    for kz in range(nz):
        for kx in range(nx):
            at = (minus(z, kz, nz) * nx + minus(x, kx, nx)) * step
            w_ref[pl.ds(pl.multiple_of(at, step), step), :] = z_refs[kz][kx]
    vectors = jnp.transpose(w_ref[:, 512:640].astype(F32))
    gain = vectors[64:65]
    shift = vectors[65:66]
    gain_ref[...] = jnp.broadcast_to(gain, (8, D))
    small = vectors[64:72].astype(BF16)
    odd = k_ref[...] == 1
    sums = dot_nn(small, select_matrix(r0_ref[...], 96 * y))
    q_bias = jnp.where(odd, sums[3:4], sums[2:3])
    sums = dot_nn(small, select_matrix(r0_ref[...], 384 + 96 * y))
    v_bias = jnp.where(odd, sums[3:4], sums[2:3])
    bias = jnp.concatenate([q_bias, jnp.zeros((1, HW), F32), v_bias], axis=1)
    for k in range(NY):
        for j in range(SLOTS):
            hat, _ = normed(x_refs[k][j * BLK : (j + 1) * BLK, :].astype(F32))
            to = pl.multiple_of(meta[M_INV + k * SLOTS + j] * BLK, BLK)
            a1_ref[pl.ds(to, BLK), :] = (hat * gain + shift).astype(BF16)

    store_a1.start()

    def project(t, carry):
        rows = pl.ds(pl.multiple_of(t * 256, 256), 256)
        joined = (dot_nn(a1_ref[rows, :], w_ref[:, 0:WQ]) + bias).astype(BF16)
        for i in range(9):
            qkv_ref[i, rows, :] = joined[:, i * HD : (i + 1) * HD]
        return carry

    lax.fori_loop(0, GROWS // 256, project, 0)
    store_qkv.start()

    def head(h, carry):
        for tile in TILES:
            q0, k0, count = tile
            q = qkv_ref[h, q0 : q0 + 256, :]
            k = qkv_ref[HEADS + h, k0 : k0 + count, :]
            v = qkv_ref[2 * HEADS + h, k0 : k0 + count, :]
            scores = jnp.where(visible_mask(meta, tile), dot_nt(scaled(q), k), MASKED_SCORE)
            top = jnp.max(scores, axis=-1, keepdims=True)
            weights = jnp.exp(scores - top)
            total = jnp.sum(weights, axis=-1, keepdims=True)
            oh[h, q0 : q0 + 256, :] = dot_nn(weights.astype(BF16), v) * (1.0 / total)
            lse_ref[h, q0 : q0 + 256, :] = top + jnp.log(total)
        return carry

    lax.fori_loop(0, HEADS, head, 0)
    for k in range(NY):
        for j in range(SLOTS):
            rows = pl.ds(pl.multiple_of(meta[M_INV + k * SLOTS + j] * BLK, BLK), BLK)
            mixed = jnp.concatenate([oh[h, rows, :] for h in range(HEADS)], axis=1)
            o_refs[k][j * BLK : (j + 1) * BLK, :] = mixed.astype(BF16)
    store_a1.wait()
    store_qkv.wait()


GELU_C = float(np.sqrt(2.0 / np.pi))


def middle_a_kernel(meta, *refs):
    o_refs, refs = refs[:NY], refs[NY:]
    x_ref, cot_ref, w_hbm = refs[:3]
    scale_ref, vec, gfcb = refs[3:6]
    kept, refs = refs[6:9], refs[9:]
    m_hbm, du_hbm, g_hbm, w, g, m_s, du_s, total_s, hat2, dz, a2, a2t, sems = refs
    y = meta[M_ZXY + 2]

    def load(i, at, to, n):
        return pltpu.make_async_copy(w_hbm.at[:, pl.ds(at, n)], w.at[:, pl.ds(to, n)], sems.at[i])

    def load_fc(q):
        return load(2 + q, pl.multiple_of(C_FC + q * D, D), pl.multiple_of(q * D, D), D)

    def load_proj(q):
        return load(6 + q, pl.multiple_of(C_PROJ + q * D, D), pl.multiple_of((4 + q) * D, D), D)

    def store(source, to, i, sem):
        at = pl.ds(pl.multiple_of(i * D, D), D)
        return pltpu.make_async_copy(source.at[:, at], to.at[:, at], sems.at[sem])

    def stores(q):
        return (
            store(g, g_hbm, q, 10 + q),
            store(g, g_hbm, 4 + q, 14 + q),
            store(m_s, m_hbm, q, 18 + q),
            store(du_s, du_hbm, q, 22 + q),
        )

    firsts = [load(0, 0, 8 * D, D), load(1, C_VEC, 9 * D, 128)]
    for copy in firsts:
        copy.start()
    for q in range(4):
        load_fc(q).start()
        load_proj(q).start()
    offset = lax.broadcasted_iota(jnp.int32, (BLK, 1), 0)
    for j in range(SLOTS):
        rows = slice(j * BLK, (j + 1) * BLK)
        live = jnp.where(offset < meta[M_THR + j], 1.0, 0.0)
        dz[rows, :] = (cot_ref[rows, :].astype(F32) * live).astype(BF16)
    for copy in firsts:
        copy.wait()
    vec[...] = jnp.transpose(w[:, 9 * D : 9 * D + 128].astype(F32))
    total = x_ref[...].astype(F32) + vec[4:5, :]
    for k in range(NY):
        at = pl.ds(pl.multiple_of(minus(y, k, NY) * HW, HW), HW)
        total = total + dot_nn(o_refs[k][...], w[at, 8 * D : 9 * D])
    hat, scale = normed(total)
    scale_ref[...] = scale
    hat2[...] = hat
    acts = hat * vec[5:6, :] + vec[6:7, :]
    a2[...] = acts.astype(BF16)
    a2t[...] = jnp.transpose(acts).astype(BF16)
    total_s[...] = total + vec[7:8, :]
    sources = (total_s, hat2, dz)
    keeps = [pltpu.make_async_copy(v, kept[i], sems.at[26 + i]) for i, v in enumerate(sources)]
    for copy in keeps:
        copy.start()
    gfcb[...] = jnp.zeros_like(gfcb)

    def step(q, carry):
        load_fc(q).wait()
        load_proj(q).wait()
        at_fc = pl.ds(pl.multiple_of(q * D, D), D)
        at_p = pl.ds(pl.multiple_of((4 + q) * D, D), D)
        u = dot_nn(a2[...], w[:, at_fc]) + vec[pl.ds(8 + q, 1), :]
        t = jnp.tanh(GELU_C * (u + 0.044715 * (u * u * u)))
        m = (0.5 * u * (1.0 + t)).astype(BF16)
        slope = 0.5 * (1.0 + t) + (0.5 * GELU_C) * u * (1.0 - t * t) * (1.0 + 0.134145 * (u * u))
        du = (dot_nt(dz[...], w[:, at_p]) * slope).astype(BF16)
        m_s[:, at_fc] = m
        du_s[:, at_fc] = du
        g[:, at_p] = dot_tn(m, dz[...]).astype(BF16)
        g[:, at_fc] = dot_nn(a2t[...], du).astype(BF16)
        gfcb[pl.ds(q, 1), :] = jnp.sum(du.astype(F32), axis=0, keepdims=True)
        for copy in stores(q):
            copy.start()
        return carry

    lax.fori_loop(0, 4, step, 0)
    for q in range(4):
        for copy in stores(q):
            copy.wait()
    for copy in keeps:
        copy.wait()


def middle_b_kernel(meta, *refs):
    o_refs, refs = refs[:NY], refs[NY:]
    scale, vec, gfcb, hat2, dz, du_hbm, w_hbm, dy_ref = refs[:8]
    do_refs, refs = refs[8 : 8 + NY], refs[8 + NY :]
    rest, w, du, gw, gvec, sems = refs
    y = meta[M_ZXY + 2]
    loads = []
    for q in range(4):
        at = pl.ds(q * D, D)
        from_w = w_hbm.at[:, pl.ds(C_FC + q * D, D)]
        loads.append(pltpu.make_async_copy(du_hbm.at[:, at], du.at[:, at], sems.at[2 * q]))
        loads.append(pltpu.make_async_copy(from_w, w.at[:, at], sems.at[2 * q + 1]))
    loads.append(
        pltpu.make_async_copy(w_hbm.at[:, pl.ds(0, D)], w.at[:, pl.ds(4 * D, D)], sems.at[8])
    )
    for load in loads:
        load.start()
    gvec[...] = jnp.zeros_like(gvec)
    gvec[8:12, :] = gfcb[0:4, :]
    da2 = jnp.zeros((ROWS, D), F32)
    for q in range(4):
        loads[2 * q].wait()
        loads[2 * q + 1].wait()
        da2 = da2 + dot_nt(du[:, q * D : (q + 1) * D], w[:, q * D : (q + 1) * D])
    hat = hat2[...]
    gvec[6:7, :] = jnp.sum(da2, axis=0, keepdims=True)
    gvec[5:6, :] = jnp.sum(da2 * hat, axis=0, keepdims=True)
    dhat = da2 * vec[5:6, :]
    mean_a = jnp.mean(dhat, axis=-1, keepdims=True)
    mean_b = jnp.mean(dhat * hat, axis=-1, keepdims=True)
    dz32 = dz[...].astype(F32)
    dy = dz32 + scale[...] * (dhat - mean_a - hat * mean_b)
    dy_ref[...] = dy
    da = dy.astype(BF16)
    gvec[7:8, :] = jnp.sum(dz32, axis=0, keepdims=True)
    gvec[4:5, :] = jnp.sum(da.astype(F32), axis=0, keepdims=True)
    loads[8].wait()
    for k in range(NY):
        at = pl.ds(pl.multiple_of(minus(y, k, NY) * HW, HW), HW)
        do_refs[k][...] = dot_nt(da, w[at, 4 * D : 5 * D]).astype(BF16)
        gw[at, :] = dot_tn(o_refs[k][...], da)
    rest[:, 0:D] = gw[...].astype(BF16)
    rest[:, D : D + 128] = jnp.transpose(gvec[...]).astype(BF16)


def out_kernel(total, m_hbm, w_hbm, out_ref, m, w, sems):
    loads = []
    for q in range(4):
        at = pl.ds(q * D, D)
        from_w = w_hbm.at[:, pl.ds(C_PROJ + q * D, D)]
        loads.append(pltpu.make_async_copy(m_hbm.at[:, at], m.at[:, at], sems.at[2 * q]))
        loads.append(pltpu.make_async_copy(from_w, w.at[:, at], sems.at[2 * q + 1]))
    for load in loads:
        load.start()
    value = total[...]
    for q in range(4):
        loads[2 * q].wait()
        loads[2 * q + 1].wait()
        value = value + dot_nn(m[:, q * D : (q + 1) * D], w[:, q * D : (q + 1) * D])
    out_ref[...] = value.astype(BF16)


def hidden_order(count, r24):
    return [
        (d * 4 * r24 + q * r24, (q * count + d) * r24) for q in range(NY) for d in range(count)
    ]


def pack_kernel(count, r6, *refs):
    sources, out, wide, vec = refs[:12], refs[12], refs[13], refs[14]
    local, sems = refs[15:27], refs[27]
    loads = [
        pltpu.make_async_copy(source, local[i], sems.at[i]) for i, source in enumerate(sources)
    ]
    for load in loads:
        load.start()
    r24 = NY * r6
    rows = out.shape[0]
    out[...] = jnp.zeros_like(out)
    vec[...] = jnp.zeros_like(vec)
    for load in loads:
        load.wait()
    wq, wo, wf, wp, g1, b1, qv, ob, g2, b2, fb, pb = local
    out[0:r6, 0 : 3 * D] = wq[...]
    out[0:r6, 3 * D : 4 * D] = wo[...]
    value = wf[...].astype(F32)
    for natural, packed in hidden_order(count, r24):
        wide[:, packed : packed + r24] = value[:, natural : natural + r24]
    out[0:r6, 4 * D : 4 * D + FF] = wide[...].astype(BF16)
    value = wp[...].astype(F32)
    for i in range(r24 // rows):
        at = 4 * D + FF + i * D
        out[:, at : at + D] = value[i * rows : (i + 1) * rows, :].astype(BF16)
    vec[0:1, 0:r6] = g1[...].astype(F32)
    vec[1:2, 0:r6] = b1[...].astype(F32)
    both = qv[...].astype(F32)
    vec[2:3, 0:r6] = both[:, 0:r6]
    vec[3:4, 0:r6] = both[:, r6 : 2 * r6]
    vec[4:5, 0:r6] = ob[...].astype(F32)
    vec[5:6, 0:r6] = g2[...].astype(F32)
    vec[6:7, 0:r6] = b2[...].astype(F32)
    vec[7:8, 0:r6] = pb[...].astype(F32)
    hidden = fb[...].astype(F32)
    for i in range(r24 // rows):
        vec[8 + i : 9 + i, 0:rows] = hidden[:, i * rows : (i + 1) * rows]
    at = out.shape[1] - 128
    out[:, at : at + 128] = jnp.transpose(vec[...])[0:rows, :].astype(BF16)


def turns_kernel(n, base, meta, *refs):
    parts, outs, total = refs[: -n - 1], refs[-n - 1 : -1], refs[-1]
    value = parts[0][...].astype(F32)
    for part in parts[1:]:
        value = value + part[...].astype(F32)
    total[...] = value
    size = total.shape[0] // n
    for k in range(n):
        at = lax.rem(meta[base] + k, n) * size
        outs[k][...] = total[pl.ds(at, size)].astype(BF16)


def rows_kernel(n, r6, meta, *refs):
    parts, outs = refs[:n], refs[n:]
    total = parts[0][...].astype(F32)
    for part in parts[1:]:
        total = total + part[...].astype(F32)
    y = meta[M_ZXY + 2]
    r24, width = total.shape
    rows = outs[0].shape[0]
    i = lax.broadcasted_iota(jnp.int32, (rows, r24), 0)
    j = lax.broadcasted_iota(jnp.int32, (rows, r24), 1)
    lane = lax.broadcasted_iota(jnp.int32, (rows, 128), 1)
    value = total.astype(BF16)
    bias = value[:, D : D + 128]
    for k in range(NY):
        to = lax.rem(y + k, NY)
        chosen = jnp.where((i < r6) & (j == i + to * r6), 1.0, 0.0).astype(BF16)
        outs[k][:, 0:width] = dot_nn(chosen, value).astype(BF16)
        hidden = jnp.zeros((rows, 128), F32)
        for g in range(r24 // rows):
            group = dot_nn(jnp.where(j == i + g * rows, 1.0, 0.0).astype(BF16), bias)
            column = jnp.sum(jnp.where(lane == 8 + to, group, 0.0), axis=1, keepdims=True)
            hidden = hidden + jnp.where(lane == g, column, 0.0)
        outs[k][:, width : width + 128] = hidden.astype(BF16)


def split_kernel(r6, meta, reduced, *refs):
    outs, (blocks,) = refs[:NY], refs[NY:]
    r24 = NY * r6
    rows = outs[0].shape[0]
    y = meta[M_ZXY + 2]
    for q in range(NY):
        blocks[q] = reduced[:, FF + q * D : FF + (q + 1) * D].astype(F32)
    i = lax.broadcasted_iota(jnp.int32, (rows, r24), 0)
    j = lax.broadcasted_iota(jnp.int32, (rows, r24), 1)
    for k in range(NY):
        to = lax.rem(y + k, NY)
        chosen = jnp.where((i < r6) & (j == i + to * r6), 1.0, 0.0).astype(BF16)
        outs[k][:, 0:FF] = dot_nn(chosen, reduced[:, 0:FF]).astype(BF16)
        value = blocks[to]
        for n in range(r24 // rows):
            outs[k][:, FF + n * D : FF + (n + 1) * D] = value[n * rows : (n + 1) * rows, :].astype(
                BF16
            )


def join_kernel(count, r6, *refs):
    parts, (fc, proj) = refs[:NY], refs[NY:]
    r24 = NY * r6
    rows = parts[0].shape[0]
    total = parts[0][...].astype(F32)
    for k in range(1, NY):
        total = total + parts[k][...].astype(F32)
    for natural, packed in hidden_order(count, r24):
        fc[:, natural : natural + r24] = total[0:r6, packed : packed + r24]
    for n in range(r24 // rows):
        proj[n * rows : (n + 1) * rows, :] = total[:, FF + n * D : FF + (n + 1) * D]


def back_kernel(nc, meta, *refs):
    do_refs, refs = refs[:NY], refs[NY:]
    x_hbm, refs = refs[:NY], refs[NY:]
    qkv_ref, lse_ref, a1_hbm, w_hbm, r0_ref, k_ref, rest_hbm = refs[:7]
    dh_refs, refs = refs[7 : 7 + NY], refs[7 + NY :]
    halves, refs = refs[:nc], refs[nc:]
    doh, dq, dk, dv, dqkv, dh, gvec, gq_ref, w_ref, x_refs, a1_ref, rest, sems = refs
    pairs = [(w_hbm, w_ref), (a1_hbm, a1_ref), (rest_hbm, rest)]
    pairs += [(x_hbm[k], x_refs.at[k]) for k in range(NY)]
    loads = [pltpu.make_async_copy(a, b, sems.at[i]) for i, (a, b) in enumerate(pairs)]
    for load in loads:
        load.start()
    y = meta[M_ZXY + 2]
    for k in range(NY):
        for j in range(SLOTS):
            rows = pl.ds(pl.multiple_of(meta[M_INV + k * SLOTS + j] * BLK, BLK), BLK)
            piece = do_refs[k][j * BLK : (j + 1) * BLK, :]
            for h in range(HEADS):
                doh[h, rows, :] = piece[:, h * HD : (h + 1) * HD]
    dk[...] = jnp.zeros_like(dk)
    dv[...] = jnp.zeros_like(dv)

    def head(h, carry):
        for tile in TILES:
            q0, k0, count = tile
            q = qkv_ref[h, q0 : q0 + 256, :]
            k = qkv_ref[HEADS + h, k0 : k0 + count, :]
            v = qkv_ref[2 * HEADS + h, k0 : k0 + count, :]
            do = doh[h, q0 : q0 + 256, :]
            q = scaled(q)
            scores = jnp.where(visible_mask(meta, tile), dot_nt(q, k), MASKED_SCORE)
            probs = jnp.exp(scores - lse_ref[h, q0 : q0 + 256, :])
            dp = dot_nt(do, v)
            row_dot = jnp.sum(dp * probs, axis=-1, keepdims=True)
            ds = (probs * (dp - row_dot)).astype(BF16)
            dq[h, q0 : q0 + 256, :] = dot_nn(ds, k) * SCALE
            dk[h, k0 : k0 + count, :] += dot_tn(ds, q)
            dv[h, k0 : k0 + count, :] += dot_tn(probs.astype(BF16), do)
        return carry

    lax.fori_loop(0, HEADS, head, 0)

    for load in loads:
        load.wait()

    def join(t, carry):
        rows = pl.ds(pl.multiple_of(t * 256, 256), 256)
        parts = [dq[h, rows, :] for h in range(HEADS)]
        parts += [dk[h, rows, :] for h in range(HEADS)]
        parts += [dv[h, rows, :] for h in range(HEADS)]
        joined = jnp.concatenate(parts, axis=1).astype(BF16)
        dqkv[rows, :] = joined
        dh[rows, :] = dot_nt(joined, w_ref[:, 0:WQ])
        return carry + jnp.sum(joined.astype(F32), axis=0, keepdims=True)

    sums = lax.fori_loop(0, GROWS // 256, join, jnp.zeros((1, WQ), F32))
    gain_sum = jnp.zeros((1, D), F32)
    shift_sum = jnp.zeros((1, D), F32)
    for k in range(NY):
        for j in range(SLOTS):
            rows = pl.ds(pl.multiple_of(meta[M_INV + k * SLOTS + j] * BLK, BLK), BLK)
            here = slice(j * BLK, (j + 1) * BLK)
            value = dh[rows, :]
            hat, _ = normed(x_refs[k, here, :].astype(F32))
            gain_sum += jnp.sum(value * hat, axis=0, keepdims=True)
            shift_sum += jnp.sum(value, axis=0, keepdims=True)
            dh_refs[k][here, :] = value.astype(dh_refs[k].dtype)
    gvec[...] = jnp.zeros_like(gvec)
    gvec[64:65, :] = gain_sum
    gvec[65:66, :] = shift_sum
    q_sum = sums[:, 0:HW]
    v_sum = sums[:, 2 * HW : 3 * HW]
    odd = k_ref[...] == 1
    for i in range(2):
        keep = odd if i else jnp.logical_not(odd)
        row = jnp.zeros((8, D), F32)
        for part, start in ((q_sum, 0), (v_sum, 384)):
            value = jnp.broadcast_to(jnp.where(keep, part, 0.0), (8, HW)).astype(BF16)
            row = row + dot_nt(value, select_matrix(r0_ref[...], start + 96 * y))
        gvec[66 + i : 67 + i, :] = row[0:1]

    def grads(c, carry):
        rows = pl.ds(pl.multiple_of(c * 256, 256), 256)
        gq_ref[rows, D + 128 : D + 128 + WQ] = dot_tn(a1_ref[:, rows], dqkv[...])
        return carry

    lax.fori_loop(0, 3, grads, 0)
    gq_ref[:, 0 : D + 128] = rest[...].astype(F32)
    gq_ref[:, D + 128 + WQ :] = jnp.transpose(gvec[...])[:, 64:128]
    blocks, size = halves[0].shape[:2]
    for k in range(nc):
        core = lax.rem(meta[M_CORE] + k, nc) * size
        for i in range(blocks):
            at = pl.multiple_of(i * size * nc + core, 8)
            halves[k][i] = gq_ref[pl.ds(at, size), :].astype(BF16)


def end_kernel(*refs):
    dh_refs = refs[:NY]
    x_ref, dy_ref, gain_ref, out_ref = refs[NY:]
    dh = dh_refs[0][...]
    for k in range(1, NY):
        dh = dh + dh_refs[k][...].astype(F32)
    hat, scale = normed(x_ref[...].astype(F32))
    dhat = dh * gain_ref[0:1, :]
    mean_a = jnp.mean(dhat, axis=-1, keepdims=True)
    mean_b = jnp.mean(dhat * hat, axis=-1, keepdims=True)
    out_ref[...] = (dy_ref[...] + scale * (dhat - mean_a - hat * mean_b)).astype(BF16)


def params(mib):
    return pltpu.CompilerParams(vmem_limit_bytes=mib * 2**20)


VMEM = pl.BlockSpec(memory_space=pltpu.VMEM)
SMEM = pl.BlockSpec(memory_space=pltpu.SMEM)
HBM = pl.BlockSpec(memory_space=pltpu.HBM)


def cost(flops, nbytes):
    return pl.CostEstimate(flops=int(flops), bytes_accessed=int(nbytes), transcendentals=0)


def on_device(
    nz,
    nx,
    nc,
    tokens,
    slot_seq,
    slot_block_index,
    lengths,
    ln1_gain,
    ln1_bias,
    w_qkv,
    qv_bias,
    w_out,
    out_bias,
    ln2_gain,
    ln2_bias,
    w_fc,
    feed_input_bias,
    w_proj,
    proj_bias,
    cotangent,
):
    r6 = w_qkv.shape[0]
    r24 = NY * r6
    count = nz * nx * nc
    y = lax.axis_index("seq")
    f = lax.axis_index("fsdp")
    z, x, c = f // (nx * nc), (f // nc) % nx, f % nc

    def shift_y(value, k):
        return lax.ppermute(value, "seq", [(i, (i + k) % NY) for i in range(NY)])

    def shift_f(value, dz, dx, dc):
        pairs = []
        for i in range(count):
            iz, ix, ic = i // (nx * nc), (i // nc) % nx, i % nc
            to = (((iz + dz) % nz) * nx + (ix + dx) % nx) * nc + (ic + dc) % nc
            pairs.append((i, to))
        return lax.ppermute(value, "fsdp", pairs)

    def pick(value, i, axis=0):
        return lax.dynamic_index_in_dim(value, i, axis, keepdims=False)

    rel = np.arange(GSLOTS)
    absolute = ((y - rel // SLOTS) % NY) * SLOTS + rel % SLOTS
    chosen = absolute[:, None] == np.arange(GSLOTS)[None, :]
    seqs = jnp.sum(jnp.where(chosen, slot_seq[None, :], 0), axis=1)
    blocks = jnp.sum(jnp.where(chosen, slot_block_index[None, :], 0), axis=1)
    lens = jnp.sum(
        jnp.where(seqs[:, None] == np.arange(lengths.shape[1])[None, :], lengths[0:1, :], 0), axis=1
    )
    order = jnp.where(lens == LONG_LEN, 0, (seqs + 1) * 16) + blocks
    inverse = jnp.sum((order[None, :] < order[:, None]).astype(jnp.int32), axis=1)
    short = inverse[None, :] == (LONG + np.arange(4))[:, None]
    codes = jnp.sum(jnp.where(short, (seqs * SEQ_STRIDE + blocks * BLK)[None, :], 0), axis=1)
    bases = jnp.sum(jnp.where(short, (seqs * SEQ_STRIDE)[None, :], 0), axis=1)
    limits = jnp.sum(jnp.where(short, (seqs * SEQ_STRIDE + lens)[None, :], 0), axis=1)
    place = jnp.stack([z, x, y]).astype(jnp.int32)
    alive = (lens - blocks * BLK)[:SLOTS]
    core = jnp.stack([c, jnp.zeros_like(c)]).astype(jnp.int32)
    meta = jnp.concatenate([inverse, codes, bases, limits, place, alive, core])
    lane = np.arange(HW)
    r0 = jnp.asarray(((lane // (2 * r6)) * r6 + lane % r6)[None, :], jnp.int32)
    kk = jnp.asarray(((lane // r6) % 2)[None, :], jnp.int32)

    rows8 = (r6 + 7) // 8 * 8
    groups = r24 // rows8
    width = 4 * D + FF + groups * D + 128
    vectors = (ln1_gain, ln1_bias, qv_bias, out_bias, ln2_gain, ln2_bias, feed_input_bias, proj_bias)
    sources = [w_qkv, w_out, w_fc, w_proj] + [v[None, :] for v in vectors]
    payload = pl.pallas_call(
        lambda *refs: pack_kernel(count, r6, *refs),
        in_specs=[HBM] * 12,
        out_specs=VMEM,
        out_shape=jax.ShapeDtypeStruct((rows8, width), BF16),
        scratch_shapes=[pltpu.VMEM((r6, FF), F32), pltpu.VMEM((128, max(128, rows8)), F32)]
        + [pltpu.VMEM(v.shape, BF16) for v in sources]
        + [pltpu.SemaphoreType.DMA((12,))],
        compiler_params=params(60),
        name="pack",
    )(*sources)
    payloads = [payload] + [shift_y(payload, k) for k in range(1, NY)]
    later, _ = lax.optimization_barrier((tokens, payload))
    token_parts = [tokens] + [shift_y(later, k) for k in range(1, NY)]
    spread = jnp.stack(payloads)
    spread = jnp.concatenate([pick(spread, (y - q) % NY)[None] for q in range(NY)])
    v0 = width - 128
    vec_rows = spread[:, :r6, v0 : v0 + 8].reshape(r24, 8)
    qkv_mine = pick(spread[:, :r6, : 3 * D].reshape(r24, 3, NY, HW), y, 2).reshape(r24, WQ)
    wq_local = jnp.concatenate([qkv_mine, vec_rows, jnp.zeros((r24, 56), BF16)], axis=1)
    proj_rows = jnp.concatenate(
        [
            jnp.concatenate(
                [
                    spread[q, :, 4 * D + FF + n * D : 4 * D + FF + (n + 1) * D]
                    for n in range(groups)
                ],
                axis=0,
            )
            for q in range(NY)
        ],
        axis=1,
    )
    fcb_rows = jnp.transpose(spread[:, :, v0 + 8 : v0 + 8 + groups], (2, 1, 0)).reshape(r24, NY)
    w_local = jnp.concatenate(
        [
            spread[:, :r6, 3 * D : 4 * D + FF].reshape(r24, D + FF),
            proj_rows,
            vec_rows,
            fcb_rows,
            jnp.zeros((r24, 116), BF16),
        ],
        axis=1,
    )
    weights = lax.all_gather(w_local, "fsdp", axis=0, tiled=True)

    pair = wq_local
    if nc == 2:
        other = shift_f(wq_local, 0, 0, 1)
        first = jnp.where(c == 0, wq_local, other)
        second = jnp.where(c == 0, other, wq_local)
        pair = jnp.concatenate([first, second], axis=0)
    line = jnp.stack([pair] + [shift_f(pair, 0, k, 0) for k in range(1, nx)])
    planes = [line] + [shift_f(line, k, 0, 0) for k in range(1, nz)]

    front = pl.pallas_call(
        lambda *refs: front_kernel(nz, nx, *refs),
        in_specs=[SMEM] + [VMEM] * (NY + nz + 2),
        out_specs=[HBM] * 2 + [VMEM] * (3 + NY),
        out_shape=[
            jax.ShapeDtypeStruct((GROWS, D), BF16),
            jax.ShapeDtypeStruct((9, GROWS, HD), BF16),
            jax.ShapeDtypeStruct((HEADS, GROWS, 1), F32),
        ]
        + [jax.ShapeDtypeStruct((ROWS, HW), BF16)] * NY
        + [jax.ShapeDtypeStruct((D, QCOLS), BF16), jax.ShapeDtypeStruct((8, D), F32)],
        scratch_shapes=[
            pltpu.VMEM((HEADS, GROWS, HD), F32),
            pltpu.VMEM((GROWS, D), BF16),
            pltpu.VMEM((9, GROWS, HD), BF16),
            pltpu.SemaphoreType.DMA((2,)),
        ],
        compiler_params=params(60),
        cost_estimate=cost(8e9, 15e6),
        name="front",
    )(meta, *token_parts, *planes, r0, kk)
    acts, qkv, lse = front[:3]
    mixed = front[3 : 3 + NY]
    wq, gain_one = front[3 + NY :]

    mixed_parts = [mixed[0]] + [shift_y(mixed[NY - k], k) for k in range(1, NY)]
    wide32 = jax.ShapeDtypeStruct((ROWS, D), F32)
    wide16 = jax.ShapeDtypeStruct((ROWS, D), BF16)
    hidden16 = jax.ShapeDtypeStruct((ROWS, FF), BF16)
    middle = pl.pallas_call(
        middle_a_kernel,
        in_specs=[SMEM] + [VMEM] * (NY + 2) + [HBM],
        out_specs=[VMEM] * 3 + [HBM] * 6,
        out_shape=[
            jax.ShapeDtypeStruct((ROWS, 1), F32),
            jax.ShapeDtypeStruct((128, D), F32),
            jax.ShapeDtypeStruct((8, D), F32),
            wide32,
            wide32,
            wide16,
            hidden16,
            hidden16,
            jax.ShapeDtypeStruct((D, 8 * D), BF16),
        ],
        scratch_shapes=[
            pltpu.VMEM((D, 9 * D + 128), BF16),
            pltpu.VMEM((D, 8 * D), BF16),
            pltpu.VMEM((ROWS, FF), BF16),
            pltpu.VMEM((ROWS, FF), BF16),
            pltpu.VMEM((ROWS, D), F32),
            pltpu.VMEM((ROWS, D), F32),
            pltpu.VMEM((ROWS, D), BF16),
            pltpu.VMEM((ROWS, D), BF16),
            pltpu.VMEM((D, ROWS), BF16),
            pltpu.SemaphoreType.DMA((29,)),
        ],
        compiler_params=params(60),
        cost_estimate=cost(8e9, 28e6),
        name="middle_a",
    )(meta, *mixed_parts, tokens, cotangent, weights)
    scale2, vec2, gfcb, total2, hat2, dz2, hidden_m, hidden_du, made_a = middle
    reduced_a = lax.psum_scatter(made_a, "fsdp", scatter_dimension=0, tiled=True)
    reduced_a = lax.optimization_barrier(reduced_a)
    middle_b = pl.pallas_call(
        middle_b_kernel,
        in_specs=[SMEM] + [VMEM] * (NY + 5) + [HBM] * 2,
        out_specs=[VMEM] * (2 + NY),
        out_shape=[wide32]
        + [jax.ShapeDtypeStruct((ROWS, HW), BF16)] * NY
        + [jax.ShapeDtypeStruct((D, D + 128), BF16)],
        scratch_shapes=[
            pltpu.VMEM((D, 5 * D), BF16),
            pltpu.VMEM((ROWS, FF), BF16),
            pltpu.VMEM((D, D), F32),
            pltpu.VMEM((128, D), F32),
            pltpu.SemaphoreType.DMA((9,)),
        ],
        compiler_params=params(60),
        cost_estimate=cost(3e9, 16e6),
        name="middle_b",
    )(meta, *mixed_parts, scale2, vec2, gfcb, hat2, dz2, hidden_du, weights)
    middle_grad = middle_b[0]
    do_made = middle_b[1 : 1 + NY]

    do_parts = [do_made[0]] + [shift_y(do_made[NY - k], k) for k in range(1, NY)]
    late_m, _ = lax.optimization_barrier((hidden_m, middle_b[1 + NY]))
    block_out = pl.pallas_call(
        out_kernel,
        in_specs=[VMEM] + [HBM] * 2,
        out_specs=VMEM,
        out_shape=wide16,
        scratch_shapes=[
            pltpu.VMEM((ROWS, FF), BF16),
            pltpu.VMEM((D, 4 * D), BF16),
            pltpu.SemaphoreType.DMA((8,)),
        ],
        compiler_params=params(60),
        cost_estimate=cost(2e9, 9e6),
        name="out",
    )(total2, late_m, weights)
    middle_rest, block_out = lax.optimization_barrier((middle_b[1 + NY], block_out))
    rest_cols = D + 128 + QCOLS
    back = pl.pallas_call(
        lambda *refs: back_kernel(nc, *refs),
        in_specs=[SMEM] + [VMEM] * NY + [HBM] * NY + [VMEM] * 2 + [HBM] * 2 + [VMEM] * 2 + [HBM],
        out_specs=[VMEM] * (NY + nc),
        out_shape=[jax.ShapeDtypeStruct((ROWS, D), F32)]
        + [jax.ShapeDtypeStruct((ROWS, D), BF16)] * (NY - 1)
        + [jax.ShapeDtypeStruct((nz * nx, r24, rest_cols), BF16)] * nc,
        scratch_shapes=[
            pltpu.VMEM((HEADS, GROWS, HD), BF16),
            pltpu.VMEM((HEADS, GROWS, HD), F32),
            pltpu.VMEM((HEADS, GROWS, HD), F32),
            pltpu.VMEM((HEADS, GROWS, HD), F32),
            pltpu.VMEM((GROWS, WQ), BF16),
            pltpu.VMEM((GROWS, D), F32),
            pltpu.VMEM((128, D), F32),
            pltpu.VMEM((D, rest_cols), F32),
            pltpu.VMEM((D, QCOLS), BF16),
            pltpu.VMEM((NY, ROWS, D), BF16),
            pltpu.VMEM((GROWS, D), BF16),
            pltpu.VMEM((D, D + 128), BF16),
            pltpu.SemaphoreType.DMA((7,)),
        ],
        compiler_params=params(60),
        cost_estimate=cost(12e9, 20e6),
        name="back",
    )(meta, *do_parts, *token_parts, qkv, lse, acts, wq, r0, kk, middle_rest)
    dh_made = back[:NY]
    dh_parts = [dh_made[0]] + [shift_y(dh_made[NY - k], k) for k in range(1, NY)]

    def turns(parts, n, base, size):
        total = parts[0].shape
        return pl.pallas_call(
            lambda *refs: turns_kernel(n, base, *refs),
            in_specs=[SMEM] + [VMEM] * len(parts),
            out_specs=[VMEM] * n,
            out_shape=[jax.ShapeDtypeStruct((total[0] // n,) + total[1:], BF16)] * n,
            scratch_shapes=[pltpu.VMEM(total, F32)],
            compiler_params=params(24),
            name="turns",
        )(meta, *parts)

    parts = [back[NY]]
    if nc == 2:
        parts.append(shift_f(back[NY + 1], 0, 0, 1))
    made = turns(parts, nz, M_ZXY, nx)
    parts = [made[0]] + [shift_f(made[k], k, 0, 0) for k in range(1, nz)]
    parts, dh_parts = lax.optimization_barrier((parts, dh_parts))
    made = turns(parts, nx, M_ZXY + 1, 1)
    parts = [made[0]] + [shift_f(made[k], 0, k, 0) for k in range(1, nx)]
    made = pl.pallas_call(
        lambda *refs: rows_kernel(nx, r6, *refs),
        in_specs=[SMEM] + [VMEM] * nx,
        out_specs=[VMEM] * NY,
        out_shape=[jax.ShapeDtypeStruct((rows8, rest_cols + 128), BF16)] * NY,
        compiler_params=params(16),
        name="rows",
    )(meta, *[part[0] for part in parts])
    row_parts = [made[0]] + [shift_y(made[k], k) for k in range(1, NY)]
    c_heads = D + 128
    summed = sum(part.astype(F32) for part in row_parts)
    heads = jnp.stack([part[:r6, c_heads : c_heads + WQ] for part in row_parts])
    heads = jnp.concatenate([pick(heads, (y - q) % NY)[:, None] for q in range(NY)], axis=1)
    grad_qkv = heads.reshape(r6, NY, 3, HW).transpose(0, 2, 1, 3).reshape(r6, 3 * D).astype(F32)
    vecs = summed[:r6, D : D + 8]
    tail = summed[:r6, c_heads + WQ : c_heads + WQ + 4]
    grad_fcb = summed[:, rest_cols : rest_cols + groups].T.reshape(r24)
    tokens_grad = pl.pallas_call(
        end_kernel,
        in_specs=[VMEM] * (NY + 3),
        out_specs=VMEM,
        out_shape=jax.ShapeDtypeStruct((ROWS, D), BF16),
        compiler_params=params(24),
        cost_estimate=cost(1e7, 6e6),
        name="end",
    )(*dh_parts, tokens, middle_grad, gain_one)

    packed = jax.ShapeDtypeStruct((rows8, FF + groups * D), BF16)
    parts = pl.pallas_call(
        lambda *refs: split_kernel(r6, *refs),
        in_specs=[SMEM, VMEM],
        out_specs=[VMEM] * NY,
        out_shape=[packed] * NY,
        scratch_shapes=[pltpu.VMEM((NY, r24, D), F32)],
        compiler_params=params(60),
        name="split",
    )(meta, reduced_a)
    parts = [parts[0]] + [shift_y(parts[k], k) for k in range(1, NY)]
    grad_fc, grad_proj = pl.pallas_call(
        lambda *refs: join_kernel(count, r6, *refs),
        in_specs=[VMEM] * NY,
        out_specs=[VMEM] * 2,
        out_shape=[jax.ShapeDtypeStruct((r6, FF), F32), jax.ShapeDtypeStruct((r24, D), F32)],
        compiler_params=params(16),
        name="join",
    )(*parts)
    return (
        block_out,
        tokens_grad,
        tail[:, 0],
        tail[:, 1],
        grad_qkv,
        tail[:, 2:4].T.reshape(2 * r6),
        summed[:r6, :D],
        vecs[:, 4],
        vecs[:, 5],
        vecs[:, 6],
        grad_fc,
        grad_fcb,
        grad_proj,
        vecs[:, 7],
    )


def solution(mesh):
    both = P(("fsdp", "seq"))
    wide = P(("fsdp", "seq"), None)
    nz, nx, nc = (4, 4, 2) if mesh.shape["fsdp"] == 32 else (1, 1, mesh.shape["fsdp"])
    in_specs = (wide, P("fsdp"), P("fsdp"), P("fsdp", None), both, both, wide, both, wide)
    in_specs += (both, both, both, wide, both, wide, both, wide)
    out_specs = (wide, wide, both, both, wide, both, wide, both, both, both, wide, both, wide, both)

    def program(*args):
        return on_device(nz, nx, nc, *args)

    return jax.shard_map(
        program, mesh=mesh, in_specs=in_specs, out_specs=out_specs, check_vma=False
    )
```
